512 devices in a mesh: dp: 16 (over y_lo, x, core), tensor: 32 (over y_hi, z).
Axes of the slice: x: 4, y: 4 (y_hi: 2, y_lo: 2; y = y_hi * 2 + y_lo), z: 16, core: 2. Of those that a mesh axis runs over, the one named last changes fastest.
Arguments:
- tokens: bfloat16 [4096, 12288], P('dp', 'tensor'), may hold values from -6 to 6
- w_blocks: bfloat16 [192, 1536, 128], P('tensor'), may hold values from -0.15625 to 0.15625
- pattern: int32 [192, 12], P('tensor'), may hold values from 0 to 95, as said below
- low_left: bfloat16 [12288, 256], P('tensor'), may hold values from -0.0546875 to 0.0546875
- low_right: bfloat16 [256, 24576], P(None, 'tensor'), may hold values from -0.375 to 0.375
- grad_out: bfloat16 [4096, 24576], P('dp', 'tensor'), may hold values from -6 to 6
Outputs:
- hidden: bfloat16 [4096, 24576], P('dp', 'tensor')
- grad_tokens: float32 [4096, 12288], P('dp', 'tensor')
- grad_blocks: float32 [192, 1536, 128], P('tensor', 'dp')
- grad_left: float32 [12288, 256], P('tensor', 'dp')
- grad_right: float32 [256, 24576], P('dp', 'tensor')
The draws below stay inside these ranges and needn't reach their ends.
Inputs may be any that keep to these rules, and one draw needn't show every extreme that they name: Each row pattern[j] holds 12 distinct block rows. With n the tensor axis's size, m = 12288 / (128 * n) block rows to a shard of the features and s = j // (24576 / (128 * n)) the shard holding block column j, every entry lies in feature shard s or in shard s XOR 2**k for some k, and one entry of the row is s m + (j mod m).
All inputs are finite; a program needn't handle non-finite values.
Results may differ from the reference program's by a relative error of at most 0.023.
Values may be sent and summed in bfloat16 or wider, within the bound.
A program may use at most 64 MiB of HBM per device.

```python
import math
import jax
import jax.numpy as jnp
from jax import lax

BLOCK = 128
D = 12288
FF = 24576
RANK = 256
TOK = 256
TOKENS = 4096
DBLK = 96
FBLK = 192
NNZ = 12
N_DP = 16
N_TENSOR = 32


def draw_pattern(key, part):
    key = jax.random.fold_in(key, 17)
    levels_count = int(N_TENSOR).bit_length() - 1
    shard_blocks = D // BLOCK // N_TENSOR
    block_cols = FF // BLOCK
    col_shard = block_cols // N_TENSOR
    cand_count = (levels_count + 1) * shard_blocks
    column_ids = jnp.arange(block_cols, dtype=jnp.int32)
    owners = column_ids // col_shard
    cand_ids = jnp.arange(cand_count, dtype=jnp.int32)
    level_of = cand_ids // shard_blocks
    inner_block = cand_ids % shard_blocks
    bit_mask = jnp.where(level_of > 0, jnp.left_shift(jnp.int32(1), jnp.maximum(level_of - 1, 0)), 0).astype(jnp.int32)
    sources = jnp.bitwise_xor(owners[:, None], bit_mask[None, :])
    global_rows = sources * shard_blocks + inner_block[None, :]
    scores = jax.random.randint(key, (block_cols, cand_count), 0, 1 << 20, dtype=jnp.int32) * cand_count + cand_ids[None, :]
    own_cand = column_ids % shard_blocks
    scores = jnp.where(cand_ids[None, :] == own_cand[:, None], -1, scores)
    _, picked = lax.top_k(-scores, NNZ)
    return jnp.take_along_axis(global_rows, picked, axis=1).astype(jnp.int32)


def steps_of(own_key, shape, pieces, low, top_value):
    level, own = 1.0, jax.random.fold_in(own_key, 6)
    for position, shards_of in pieces:
        draws = jnp.exp(jax.random.uniform(jax.random.fold_in(own, position), (shards_of,), jnp.float32, low / len(pieces), top_value / len(pieces)))
        level = level * jnp.repeat(draws, shape[position] // shards_of).reshape([-1 if axis == position else 1 for axis in range(len(shape))])
    return level


def centred(stream_key, extent, width, bound, pieces=(), kind=jnp.bfloat16):
    gain = steps_of(stream_key, extent, pieces, -0.22, 0.18) if pieces else 1.0
    drawn = jax.random.normal(stream_key, extent, jnp.float32) * width * gain
    return jnp.minimum(jnp.maximum(drawn, -bound), bound).astype(kind)


def setup_inputs(seed: int = 0) -> dict:
    keys = jax.random.split(jax.random.key(seed), 7)
    return {
        "tokens": centred(keys[0], (TOKENS, D), 1.0, 6.0, ((0, 16), (1, 32))),
        "w_blocks": centred(keys[1], (FBLK, NNZ * BLOCK, BLOCK), (NNZ * BLOCK) ** -0.5, 0.15625, ((0, 32),)),
        "pattern": draw_pattern(jax.random.fold_in(keys[6], 71), 0),
        "low_left": centred(keys[3], (D, RANK), D ** -0.5, 0.0546875, ((0, 32),)),
        "low_right": centred(keys[4], (RANK, FF), RANK ** -0.5, 0.375, ((1, 32),)),
        "grad_out": centred(keys[5], (TOKENS, FF), 1.0, 6.0, ((0, 16), (1, 32))),
    }


def gelu_pair(pre_act, grad_out):
    activated, pullback = jax.vjp(jax.nn.gelu, pre_act)
    return (activated, pullback(grad_out.astype(jnp.float32))[0])

def group_sum(partials):
    rounded = lax.optimization_barrier(partials.astype(jnp.bfloat16))
    return lax.optimization_barrier(jnp.sum(rounded.astype(jnp.float32), axis=0))

def reference(tokens, w_blocks, pattern, low_left, low_right, grad_out):
    feature_blocks = tokens.reshape(TOKENS, DBLK, BLOCK)
    low_codes = jnp.dot(tokens, low_left, preferred_element_type=jnp.float32).astype(jnp.bfloat16)

    def forward_column(column):
        weight, block_rows = column
        picked = jnp.take(feature_blocks, block_rows, axis=1).reshape(TOKENS, NNZ * BLOCK)
        return jnp.dot(picked, weight, preferred_element_type=jnp.float32)
    sparse_part = lax.map(forward_column, (w_blocks, pattern))
    sparse_part = jnp.transpose(sparse_part, (1, 0, 2)).reshape(TOKENS, FF)
    pre_act = sparse_part + jnp.dot(low_codes, low_right, preferred_element_type=jnp.float32)
    hidden_full, grad_full = gelu_pair(pre_act, grad_out)
    hidden = hidden_full.astype(jnp.bfloat16)
    pre_grad = grad_full.astype(jnp.bfloat16)
    back_codes = jnp.dot(pre_grad, low_right.T, preferred_element_type=jnp.float32).astype(jnp.bfloat16)
    grad_columns = jnp.transpose(pre_grad.reshape(TOKENS, FBLK, BLOCK), (1, 0, 2))

    def backward_column(carry, column):
        weight, block_rows, grad_block = column
        product = jnp.dot(grad_block, weight.T, preferred_element_type=jnp.float32).reshape(TOKENS, NNZ, BLOCK)
        return (carry.at[:, block_rows].add(product), None)
    start = jnp.zeros((TOKENS, DBLK, BLOCK), jnp.float32)
    accumulated, _ = lax.scan(backward_column, start, (w_blocks, pattern, grad_columns))
    grad_tokens = accumulated.reshape(TOKENS, D) + jnp.dot(back_codes, low_left.T, preferred_element_type=jnp.float32)
    grad_scale = 1.0 / math.sqrt(TOKENS)

    def weight_column(column):
        block_rows, grad_block = column
        picked = jnp.take(feature_blocks, block_rows, axis=1).reshape(N_DP, TOK, NNZ * BLOCK).astype(jnp.float32)
        grads = grad_block.reshape(N_DP, TOK, BLOCK).astype(jnp.float32)
        return group_sum(jnp.einsum('cti,cto->cio', picked, grads) * grad_scale)
    grad_blocks = lax.map(weight_column, (pattern, grad_columns))
    group_tokens = tokens.reshape(N_DP, TOK, D).astype(jnp.float32)
    group_back = back_codes.reshape(N_DP, TOK, RANK).astype(jnp.float32)
    grad_left = group_sum(jnp.einsum('cti,ctr->cir', group_tokens, group_back) * grad_scale)
    group_codes = low_codes.reshape(N_DP, TOK, RANK).astype(jnp.float32)
    group_grads = pre_grad.reshape(N_DP, TOK, FF).astype(jnp.float32)
    grad_right = group_sum(jnp.einsum('ctr,cto->cro', group_codes, group_grads) * grad_scale)
    return (hidden, grad_tokens, grad_blocks, grad_left, grad_right)
```

```python
import functools
import math

import jax
import jax.numpy as jnp
from jax import lax
from jax.experimental import pallas as pl
from jax.experimental.pallas import tpu as pltpu
from jax.sharding import PartitionSpec as P

MESH = pl.DeviceIdType.MESH
BF, F32 = jnp.bfloat16, jnp.float32
BLOCK = 128
NNZ = 12
TOK = 256
MB = 3
COLS = 6
LEVELS = 6
SLOTS = MB * LEVELS
RANK = 256
HID = COLS * BLOCK
FEAT = MB * BLOCK
CHUNKS = 6
GROUPS = 2
GCOLS = COLS // GROUPS
CHIPS = 8
TENSOR_PEERS = (1, 2, 4, 12, 16)
CHIP_MASKS = tuple(range(1, CHIPS))
GELU_C = math.sqrt(2.0 / math.pi)
GELU_A = 0.044715


def dot(a, b):
    return jnp.dot(a, b, preferred_element_type=F32)


class Sems:
    def __init__(self, send, recv):
        self.send, self.recv, self.used = send, recv, 0

    def copy(self, src, dst, **device):
        i = self.used
        self.used += 1
        return pltpu.make_async_remote_copy(
            src_ref=src, dst_ref=dst, send_sem=self.send.at[i], recv_sem=self.recv.at[i],
            device_id=device, device_id_type=MESH,
        )


NUM_SEMS = 160


def kernel(
    grad_scale, tokens, w, pat, left, right, gout,
    hidden, gtok, gblk, glt, gright,
    cand, cand_t, wd, wd_t, pre, pg, left_t, right_t,
    acc, stage128, stage64, stage32, stage16, stagec,
    rb128, rb64, rb32, rb16, rbc, rc128, rc64, rc32, rc16, rcc,
    codes, back, gsend, rx, g4, g0,
    tb, tb_rc, tb_s, tb_r, tr, tr_rc, tr_s, tr_r, tl, tl_rc, tl_s, tl_r,
    send_sem, recv_sem,
):
    s = lax.axis_index("tensor")
    d = lax.axis_index("dp")
    core = lax.rem(d, 2)
    chip = d // 2
    other = 1 - core
    sems = Sems(send_sem, recv_sem)
    pending = []

    def launch(src, dst, **device):
        c = sems.copy(src, dst, **device)
        c.start()
        pending.append(c)
        return c

    barrier = pltpu.get_barrier_semaphore()
    for m in TENSOR_PEERS:
        pl.semaphore_signal(barrier, inc=1, device_id={"tensor": s ^ m}, device_id_type=MESH)
    pl.semaphore_signal(barrier, inc=1, device_id={"dp": d ^ 1}, device_id_type=MESH)
    for m in CHIP_MASKS:
        pl.semaphore_signal(barrier, inc=1, device_id={"dp": d ^ (2 * m)}, device_id_type=MESH)
    for i in range(MB):
        cand[i] = tokens[:, i * BLOCK : (i + 1) * BLOCK]
    pl.semaphore_wait(barrier, len(TENSOR_PEERS) + 1 + len(CHIP_MASKS))

    def part(c):
        i, h = c // 2, c % 2
        return i, pl.ds(h * 128, 128)

    four = []
    for c in range(CHUNKS):
        i, rows = part(c)
        four.append(launch(cand.at[i, rows], cand.at[9 + i, rows], tensor=s ^ 4))
    own = cand.at[pl.ds(0, MB)]
    sixteen = launch(own, cand.at[pl.ds(15, MB)], tensor=s ^ 16)
    two = launch(own, cand.at[pl.ds(6, MB)], tensor=s ^ 2)
    one = launch(own, cand.at[pl.ds(3, MB)], tensor=s ^ 1)
    relayed = []

    def relay(c):
        i, rows = part(c)
        four[c].wait_recv()
        relayed.append(launch(cand.at[9 + i, rows], cand.at[12 + i, rows], tensor=s ^ 12))

    bit = lambda n: lax.rem(lax.shift_right_logical(s, n), 2)
    b16, b1, b2, b3 = bit(4), bit(0), bit(1), bit(3)
    b4 = bit(2) ^ b3
    off = [0]
    for b, h in ((b16, 128), (b1, 64), (b2, 32), (b4, 16)):
        off.append(off[-1] + b * h)
    col = pl.multiple_of(b3 * 128, 128)
    row_steps = ((16, b16, 128, stage128), (1, b1, 64, stage64), (2, b2, 32, stage32), (4, b4, 16, stage16))

    def rows_at(start, size):
        return pl.ds(pl.multiple_of(start, 16), size)

    class AllReduce:
        def __init__(self, bufs, out):
            self.bufs, self.out, self.flying = bufs, out, None

        def scatter_send(self, i):
            if i < 4:
                mask, b, h, stage = row_steps[i]
                stage[...] = acc[rows_at(off[i] + (1 - b) * h, h), :].astype(BF)
            else:
                mask, stage = 12, stagec
                ocol = pl.multiple_of((1 - b3) * 128, 128)
                stage[...] = acc[rows_at(off[4], 16), pl.ds(ocol, 128)].astype(BF)
            self.flying = launch(stage, self.bufs[i], tensor=s ^ mask)

        def scatter_recv(self, i):
            self.flying.wait()
            pending[:] = [c for c in pending if c is not self.flying]
            if i < 4:
                h = row_steps[i][2]
                keep = rows_at(off[i + 1], h)
                acc[keep, :] = acc[keep, :] + self.bufs[i][...].astype(F32)
            else:
                keep = rows_at(off[4], 16)
                self.out[keep, pl.ds(col, 128)] = (
                    acc[keep, pl.ds(col, 128)] + self.bufs[4][...].astype(F32)
                ).astype(BF)

        def gather_send(self, i):
            if i == 0:
                view, mask = self.out.at[rows_at(off[4], 16), pl.ds(col, 128)], 12
            else:
                k = 4 - i
                mask, _, h, _ = row_steps[k]
                view = self.out.at[rows_at(off[k + 1], h)]
            self.flying = launch(view, view, tensor=s ^ mask)

        def gather_recv(self):
            self.flying.wait_recv()

        def step(self, n):
            if n < 5:
                self.scatter_recv(n)
                if n < 4:
                    self.scatter_send(n + 1)
                else:
                    self.gather_send(0)
            else:
                self.gather_recv()
                if n < 9:
                    self.gather_send(n - 4)

    ar = AllReduce((rb128, rb64, rb32, rb16, rbc), codes)
    acc[...] = dot(tokens[...], left[...])
    ar.scatter_send(0)

    def dense(first, last):
        def body(slot, carry):
            level = slot // MB
            mask = lax.shift_right_logical(lax.shift_left(jnp.int32(1), level), 1)
            row = (s ^ mask) * MB + lax.rem(slot, MB)
            for j in range(COLS):
                k = jnp.int32(0)
                found = jnp.int32(0)
                for q in range(NNZ):
                    hit = pat[j, q] == row
                    k = jnp.where(hit, q, k)
                    found = jnp.where(hit, 1, found)
                block = jnp.where(found > 0, w[j, k], jnp.zeros((BLOCK, BLOCK), BF))
                wd[slot, :, j * BLOCK : (j + 1) * BLOCK] = block
                wd_t[slot, j * BLOCK : (j + 1) * BLOCK, :] = block.T
            return carry

        lax.fori_loop(first, last, body, 0)

    def turned(first, last):
        def body(slot, carry):
            cand_t[slot] = cand[slot].T
            return carry

        lax.fori_loop(first, last, body, 0)

    def forward(slots, start=None):
        def body(n, carry):
            columns = pl.ds(pl.multiple_of(n * 256, 256), 256)
            total = start(columns) if start is not None else pre[:, columns]
            for p in range(0, len(slots), 2):
                pair = slots[p : p + 2]
                x = jnp.concatenate([cand[q] for q in pair], axis=1)
                y = jnp.concatenate([wd[q, :, columns] for q in pair], axis=0)
                total = total + dot(x, y)
            pre[:, columns] = total
            return carry

        lax.fori_loop(0, HID // 256, body, 0)

    dense(0, 6)
    ar.step(0)
    dense(6, 12)
    ar.step(1)
    relay(0)
    dense(12, 18)
    ar.step(2)
    relay(1)
    left_t[...] = left[...].T
    right_t[...] = right[...].T
    turned(0, 3)
    ar.step(3)
    relay(2)
    sixteen.wait_recv()
    turned(15, 18)
    ar.step(4)
    relay(3)
    one.wait_recv()
    two.wait_recv()
    turned(3, 9)
    ar.step(5)
    relay(4)
    ar.step(6)
    relay(5)
    forward((0, 1, 2, 15, 16, 17, 3, 4, 5, 6, 7, 8), lambda columns: jnp.zeros((TOK, 256), F32))
    ar.step(7)
    turned(9, 12)
    forward((9, 10, 11))
    ar.step(8)
    for c in range(CHUNKS):
        relayed[c].wait_recv()
        if c == 3:
            ar.step(9)
    turned(12, 15)

    def activate(n, carry):
        columns = pl.ds(pl.multiple_of(n * 256, 256), 256)
        u = pre[:, columns]
        u = u + dot(jnp.concatenate([cand[12], cand[13]], axis=1),
                    jnp.concatenate([wd[12, :, columns], wd[13, :, columns]], axis=0))
        u = u + dot(cand[14], wd[14, :, columns])
        u = u + dot(codes[...], right[:, columns])
        uu = u * u
        t = jnp.tanh(GELU_C * (u + GELU_A * (uu * u)))
        hidden[:, columns] = (0.5 * u * (1.0 + t)).astype(BF)
        slope = 0.5 * (1.0 + t) + 0.5 * u * (1.0 - t * t) * (GELU_C * (1.0 + 3.0 * GELU_A * uu))
        pg[:, columns] = (gout[:, columns].astype(F32) * slope).astype(BF)
        return carry

    lax.fori_loop(0, HID // 256, activate, 0)

    def term(slot):
        return dot(pg[...], wd_t[slot])

    far = []
    for i in range(MB):
        gsend[12 + i] = term(12 + i).astype(BF)
        far.append(launch(gsend.at[12 + i], rx.at[12 + i], tensor=s ^ 12))
    ar = AllReduce((rc128, rc64, rc32, rc16, rcc), back)
    acc[...] = dot(pg[...], right_t[...])
    ar.scatter_send(0)

    def near(level, mask):
        def body(i, carry):
            gsend[MB * level + i] = term(MB * level + i).astype(BF)
            return carry

        lax.fori_loop(0, MB, body, 0)
        view = pl.ds(MB * level, MB)
        return launch(gsend.at[view], rx.at[view], tensor=s ^ mask)

    nears = [near(5, 16), near(2, 2), near(1, 1)]

    def g4_body(i, carry):
        g4[i] = term(9 + i)
        return carry

    lax.fori_loop(0, MB, g4_body, 0)

    def slot_of(p):
        apart = (p // MB) ^ s
        level = jnp.int32(0)
        for n in range(LEVELS - 1):
            level = level + (apart == (1 << n)).astype(jnp.int32) * (n + 1)
        return level * MB + lax.rem(p, MB)

    def blocks(group):
        def body(n, carry):
            j = group * GCOLS + n
            g = pg[:, pl.ds(pl.multiple_of(j * BLOCK, BLOCK), BLOCK)]
            for k in range(NNZ):
                x = (dot(cand_t[slot_of(pat[j, k])], g) * grad_scale).astype(BF)
                row = 0
                while row < BLOCK:
                    at = k * BLOCK + row
                    piece, inner = at // 96, at % 96
                    size = min(96 - inner, BLOCK - row)
                    tb[j, piece // 2, piece % 2, inner : inner + size, :] = x[row : row + size]
                    row += size
            return carry

        lax.fori_loop(0, GCOLS, body, 0)
        view = pl.ds(group * GCOLS, GCOLS)
        return launch(tb.at[view, :, other], tb_rc.at[view], dp=d ^ 1)

    def spread(sent, received):
        return [launch(sent(chip ^ m), received(m), dp=d ^ (2 * m)) for m in CHIP_MASKS]

    def blocks_sum(group, copy):
        copy.wait_recv()

        def body(c, carry):
            for n in range(GCOLS):
                j = group * GCOLS + n
                tb_s[group, c, n] = (tb[j, c, core].astype(F32) + tb_rc[j, c].astype(F32)).astype(BF)
            return carry

        lax.fori_loop(0, CHIPS, body, 0)
        return spread(lambda c: tb_s.at[group, c], lambda m: tb_r.at[group, m])

    def flat_sum(mine, theirs, out, copy, received):
        copy.wait_recv()

        def body(c, carry):
            out[c] = (mine[c, core].astype(F32) + theirs[c].astype(F32)).astype(BF)
            return carry

        lax.fori_loop(0, CHIPS, body, 0)
        return spread(lambda c: out.at[c], lambda m: received.at[m])

    def far_relay(i):
        far[i].wait_recv()
        gsend[9 + i] = (g4[i] + rx[12 + i].astype(F32)).astype(BF)
        return launch(gsend.at[9 + i], rx.at[9 + i], tensor=s ^ 4)

    core0 = blocks(0)
    ar.step(0)
    core1 = blocks(1)
    t = (dot(codes[...].T, pg[...]) * grad_scale).astype(BF)
    for c in range(CHIPS):
        for h in range(2):
            r = (2 * c + h) * 16
            tr[c, h] = t[r : r + 16]
    core_r = launch(tr.at[:, other], tr_rc, dp=d ^ 1)
    ar.step(1)
    eight0 = blocks_sum(0, core0)
    nears.append(far_relay(0))
    ar.step(2)
    eight1 = blocks_sum(1, core1)
    nears.append(far_relay(1))
    ar.step(3)
    eight_r = flat_sum(tr, tr_rc, tr_s, core_r, tr_r)
    nears.append(far_relay(2))
    ar.step(4)

    def g0_body(i, carry):
        g0[i] = term(i)
        return carry

    lax.fori_loop(0, MB, g0_body, 0)
    for n in range(5, 10):
        ar.step(n)
    t = (dot(back[...].T, tokens[...]) * grad_scale).astype(BF)
    for c in range(CHIPS):
        for h in range(2):
            r = (2 * c + h) * 16
            tl[c, h] = t[r : r + 16]
    core_l = launch(tl.at[:, other], tl_rc, dp=d ^ 1)
    eight_l = flat_sum(tl, tl_rc, tl_s, core_l, tl_r)

    def sum_flat(own_view, received, copies, out):
        total = own_view[...].astype(F32)
        for m, c in zip(CHIP_MASKS, copies):
            c.wait_recv()
            total = total + received[m].astype(F32)
        out[...] = total

    for group, copies in ((0, eight0), (1, eight1)):
        for c in copies:
            c.wait_recv()

        def body(n, carry, group=group):
            total = tb_s[group, chip, n].astype(F32)
            for m in CHIP_MASKS:
                total = total + tb_r[group, m, n].astype(F32)
            gblk[group * GCOLS + n] = total
            return carry

        lax.fori_loop(0, GCOLS, body, 0)
    sum_flat(tr_s.at[chip], tr_r, eight_r, gright)
    for c in nears:
        c.wait_recv()
    low = dot(back[...], left_t[...])
    for i in range(MB):
        total = g0[i] + low[:, i * BLOCK : (i + 1) * BLOCK]
        for level in (1, 2, 3, 5):
            total = total + rx[MB * level + i].astype(F32)
        gtok[:, i * BLOCK : (i + 1) * BLOCK] = total
    sum_flat(tl_s.at[chip], tl_r, eight_l, glt)
    for c in pending:
        c.wait_send()


def per_device(tokens, w_blocks, pattern, low_left, low_right, grad_out):
    grad_scale = 1.0 / math.sqrt(TOK * lax.axis_size("dp"))
    vmem = pl.BlockSpec(memory_space=pltpu.VMEM)
    smem = pl.BlockSpec(memory_space=pltpu.SMEM)
    V = pltpu.VMEM
    ar_bufs = [V((h, RANK), BF) for h in (128, 64, 32, 16)] + [V((16, 128), BF)]
    scratch = [
        V((SLOTS, TOK, BLOCK), BF), V((SLOTS, BLOCK, TOK), BF),
        V((SLOTS, BLOCK, HID), BF), V((SLOTS, HID, BLOCK), BF),
        V((TOK, HID), F32), V((TOK, HID), BF), V((RANK, FEAT), BF), V((HID, RANK), BF),
        V((TOK, RANK), F32), *ar_bufs, *ar_bufs, *ar_bufs,
        V((TOK, RANK), BF), V((TOK, RANK), BF),
        V((SLOTS, TOK, BLOCK), BF), V((SLOTS, TOK, BLOCK), BF),
        V((MB, TOK, BLOCK), F32), V((MB, TOK, BLOCK), F32),
        V((COLS, CHIPS, 2, 96, BLOCK), BF), V((COLS, CHIPS, 96, BLOCK), BF),
        V((GROUPS, CHIPS, GCOLS, 96, BLOCK), BF), V((GROUPS, CHIPS, GCOLS, 96, BLOCK), BF),
        V((CHIPS, 2, 16, HID), BF), V((CHIPS, 16, HID), BF), V((CHIPS, 16, HID), BF), V((CHIPS, 16, HID), BF),
        V((CHIPS, 2, 16, FEAT), BF), V((CHIPS, 16, FEAT), BF), V((CHIPS, 16, FEAT), BF), V((CHIPS, 16, FEAT), BF),
        pltpu.SemaphoreType.DMA((NUM_SEMS,)), pltpu.SemaphoreType.DMA((NUM_SEMS,)),
    ]
    out_shape = (
        jax.ShapeDtypeStruct((TOK, HID), BF),
        jax.ShapeDtypeStruct((TOK, FEAT), F32),
        jax.ShapeDtypeStruct((COLS, 96, BLOCK), F32),
        jax.ShapeDtypeStruct((16, FEAT), F32),
        jax.ShapeDtypeStruct((16, HID), F32),
    )
    hidden, gtok, gblk, glt, gright = pl.pallas_call(
        functools.partial(kernel, grad_scale),
        name="pixelfly",
        out_shape=out_shape,
        in_specs=[vmem, vmem, smem, vmem, vmem, vmem],
        out_specs=(vmem,) * 5,
        scratch_shapes=scratch,
        compiler_params=pltpu.CompilerParams(
            collective_id=0, has_side_effects=True, vmem_limit_bytes=48 << 20
        ),
        cost_estimate=pl.CostEstimate(flops=3 << 30, bytes_accessed=6 << 20, transcendentals=TOK * HID),
    )(tokens, w_blocks.reshape(COLS, NNZ, BLOCK, BLOCK), pattern, low_left, low_right, grad_out)
    return hidden, gtok, gblk, glt.T, gright


def solution(mesh):
    in_specs = (
        P("dp", "tensor"),
        P("tensor", None, None),
        P("tensor", None),
        P("tensor", None),
        P(None, "tensor"),
        P("dp", "tensor"),
    )
    out_specs = (
        P("dp", "tensor"),
        P("dp", "tensor"),
        P("tensor", "dp", None),
        P("tensor", "dp"),
        P("dp", "tensor"),
    )
    return jax.shard_map(
        per_device, mesh=mesh, in_specs=in_specs, out_specs=out_specs, check_vma=False
    )
```

```python
import functools
import math

import jax
import jax.numpy as jnp
from jax import lax
from jax.experimental import pallas as pl
from jax.experimental.pallas import tpu as pltpu
from jax.sharding import PartitionSpec as P

MESH = pl.DeviceIdType.MESH
BF, F32 = jnp.bfloat16, jnp.float32
BLOCK = 128
NNZ = 12
TOK = 256
MB = 3
COLS = 6
LEVELS = 6
SLOTS = MB * LEVELS
RANK = 256
HID = COLS * BLOCK
FEAT = MB * BLOCK
CHUNKS = 6
GROUPS = 2
GCOLS = COLS // GROUPS
CHIPS = 8
NEAR_GROUP = (1, 2, 3, 16, 17, 18, 19)
FAR_GROUP = (4, 8, 12)
TENSOR_PEERS = NEAR_GROUP + FAR_GROUP
CHIP_MASKS = tuple(range(1, CHIPS))
GELU_C = math.sqrt(2.0 / math.pi)
GELU_A = 0.044715


def dot(a, b):
    return jnp.dot(a, b, preferred_element_type=F32)


class Sems:
    def __init__(self, send, recv):
        self.send, self.recv, self.used = send, recv, 0

    def copy(self, src, dst, **device):
        i = self.used
        self.used += 1
        return pltpu.make_async_remote_copy(
            src_ref=src, dst_ref=dst, send_sem=self.send.at[i], recv_sem=self.recv.at[i],
            device_id=device, device_id_type=MESH,
        )


NUM_SEMS = 160


def kernel(
    grad_scale, tokens_hbm, w_hbm, pat_hbm, left_hbm, right_hbm, gout_hbm,
    hidden, gtok, gblk, glt, gright,
    w, pat, left, right, gout, load_sem,
    cand, cand_t, wd, wd_t, pre, pg, left_t, right_t,
    acc, acc2, sa_f, sa_b, sb_f, sb_b, ra_f, ra_b, rb_f, rb_b,
    codes, back, gsend, rx, g4, g0,
    tb, tb_rc, tb_s, tb_r, tr, tr_rc, tr_s, tr_r, tl, tl_rc, tl_s, tl_r,
    send_sem, recv_sem,
):
    s = lax.axis_index("tensor")
    d = lax.axis_index("dp")
    core = lax.rem(d, 2)
    chip = d // 2
    other = 1 - core
    sems = Sems(send_sem, recv_sem)
    pending = []

    def launch(src, dst, **device):
        c = sems.copy(src, dst, **device)
        c.start()
        pending.append(c)
        return c

    barrier = pltpu.get_barrier_semaphore()
    for m in TENSOR_PEERS:
        pl.semaphore_signal(barrier, inc=1, device_id={"tensor": s ^ m}, device_id_type=MESH)
    pl.semaphore_signal(barrier, inc=1, device_id={"dp": d ^ 1}, device_id_type=MESH)
    for m in CHIP_MASKS:
        pl.semaphore_signal(barrier, inc=1, device_id={"dp": d ^ (2 * m)}, device_id_type=MESH)

    def fetch(n, src, dst):
        c = pltpu.make_async_copy(src, dst, load_sem.at[n])
        c.start()
        return c

    loads = [fetch(i, tokens_hbm.at[:, pl.ds(i * BLOCK, BLOCK)], cand.at[i]) for i in range(MB)]
    loads.append(fetch(3, left_hbm, left))
    pat_load = fetch(4, pat_hbm, pat)
    w_load = fetch(5, w_hbm, w)
    right_load = fetch(6, right_hbm, right)
    gout_load = fetch(7, gout_hbm, gout)
    for c in loads:
        c.wait()

    def tokens():
        return jnp.concatenate([cand[i] for i in range(MB)], axis=1)

    acc[...] = dot(tokens(), left[...])
    sa_f[...] = acc[...].astype(BF)
    pl.semaphore_wait(barrier, len(TENSOR_PEERS) + 1 + len(CHIP_MASKS))

    def part(c):
        i, h = c // 2, c % 2
        return i, pl.ds(h * 128, 128)

    bit = lambda v, n: lax.rem(lax.shift_right_logical(v, n), 2)
    near_row = lambda v: pl.multiple_of(32 * (bit(v, 0) + 2 * bit(v, 1) + 4 * bit(v, 4)), 32)
    far_row = lambda v: pl.multiple_of(16 * bit(v, 2), 16)
    far_col = lambda v: pl.multiple_of(128 * bit(v, 3), 128)

    class AllReduce:
        def __init__(self, total, near_stage, far_stage, near_in, far_in, out):
            self.total, self.near_stage, self.far_stage = total, near_stage, far_stage
            self.near_in, self.far_in, self.out = near_in, far_in, out

        def start(self):
            self.flying = [
                launch(self.near_stage.at[pl.ds(near_row(s ^ m), 32)], self.near_in.at[n], tensor=s ^ m)
                for n, m in enumerate(NEAR_GROUP)
            ]

        def arrived(self):
            for c in self.flying:
                c.wait_recv()

        def step(self, n):
            self.arrived()
            rows = pl.ds(near_row(s), 32)
            piece = self.out.at[pl.ds(pl.multiple_of(near_row(s) + far_row(s), 16), 16), pl.ds(far_col(s), 128)]
            if n == 0:
                part = self.total[rows, :]
                for m in range(len(NEAR_GROUP)):
                    part = part + self.near_in[m].astype(F32)
                self.total[rows, :] = part
                self.far_stage[...] = part.astype(BF)
                self.flying = [
                    launch(
                        self.far_stage.at[pl.ds(far_row(s ^ m), 16), pl.ds(far_col(s ^ m), 128)],
                        self.far_in.at[i], tensor=s ^ m,
                    )
                    for i, m in enumerate(FAR_GROUP)
                ]
            elif n == 1:
                part = self.total[
                    pl.ds(pl.multiple_of(near_row(s) + far_row(s), 16), 16), pl.ds(far_col(s), 128)
                ]
                for m in range(len(FAR_GROUP)):
                    part = part + self.far_in[m].astype(F32)
                piece[...] = part.astype(BF)
                self.flying = [launch(piece, piece, tensor=s ^ m) for m in FAR_GROUP]
            elif n == 2:
                view = self.out.at[rows]
                self.flying = [launch(view, view, tensor=s ^ m) for m in NEAR_GROUP]

    four = []
    for c in range(2):
        i, rows = part(c)
        four.append(launch(cand.at[i, rows], cand.at[9 + i, rows], tensor=s ^ 4))
    ar = AllReduce(acc, sa_f, sb_f, ra_f, rb_f, codes)
    ar.start()
    for c in range(2, CHUNKS):
        i, rows = part(c)
        four.append(launch(cand.at[i, rows], cand.at[9 + i, rows], tensor=s ^ 4))
    own = cand.at[pl.ds(0, MB)]
    sixteen = launch(own, cand.at[pl.ds(15, MB)], tensor=s ^ 16)
    two = launch(own, cand.at[pl.ds(6, MB)], tensor=s ^ 2)
    one = launch(own, cand.at[pl.ds(3, MB)], tensor=s ^ 1)
    relayed = []

    def relay(c):
        i, rows = part(c)
        four[c].wait_recv()
        relayed.append(launch(cand.at[9 + i, rows], cand.at[12 + i, rows], tensor=s ^ 12))

    def dense(first, last):
        def body(slot, carry):
            level = slot // MB
            mask = lax.shift_right_logical(lax.shift_left(jnp.int32(1), level), 1)
            row = (s ^ mask) * MB + lax.rem(slot, MB)
            for j in range(COLS):
                k = jnp.int32(0)
                found = jnp.int32(0)
                for q in range(NNZ):
                    hit = pat[j, q] == row
                    k = jnp.where(hit, q, k)
                    found = jnp.where(hit, 1, found)
                block = jnp.where(found > 0, w[j, k], jnp.zeros((BLOCK, BLOCK), BF))
                wd[slot, :, j * BLOCK : (j + 1) * BLOCK] = block
                wd_t[slot, j * BLOCK : (j + 1) * BLOCK, :] = block.T
            return carry

        lax.fori_loop(first, last, body, 0)

    def turned(first, last):
        def body(slot, carry):
            cand_t[slot] = cand[slot].T
            return carry

        lax.fori_loop(first, last, body, 0)

    def forward(slots, start=None):
        def body(n, carry):
            columns = pl.ds(pl.multiple_of(n * 256, 256), 256)
            total = start(columns) if start is not None else pre[:, columns]
            for p in range(0, len(slots), 2):
                pair = slots[p : p + 2]
                x = jnp.concatenate([cand[q] for q in pair], axis=1)
                y = jnp.concatenate([wd[q, :, columns] for q in pair], axis=0)
                total = total + dot(x, y)
            pre[:, columns] = total
            return carry

        lax.fori_loop(0, HID // 256, body, 0)

    pat_load.wait()
    w_load.wait()
    dense(0, 4)
    relay(0)
    ar.step(0)
    dense(4, 8)
    relay(1)
    dense(8, 12)
    relay(2)
    ar.step(1)
    dense(12, 15)
    relay(3)
    dense(15, 18)
    right_load.wait()
    left_t[...] = left[...].T
    relay(4)
    right_t[...] = right[...].T
    turned(0, 3)
    sixteen.wait_recv()
    turned(15, 18)
    relay(5)
    ar.step(2)
    one.wait_recv()
    two.wait_recv()
    turned(3, 9)
    forward((0, 1, 2, 15, 16, 17, 3, 4, 5, 6, 7, 8), lambda columns: jnp.zeros((TOK, 256), F32))
    turned(9, 12)
    forward((9, 10, 11))
    ar.step(3)
    gout_load.wait()
    for c in range(CHUNKS):
        relayed[c].wait_recv()
    def activate(n, carry):
        columns = pl.ds(pl.multiple_of(n * 256, 256), 256)
        u = pre[:, columns]
        u = u + dot(jnp.concatenate([cand[12], cand[13]], axis=1),
                    jnp.concatenate([wd[12, :, columns], wd[13, :, columns]], axis=0))
        u = u + dot(cand[14], wd[14, :, columns])
        u = u + dot(codes[...], right[:, columns])
        uu = u * u
        t = jnp.tanh(GELU_C * (u + GELU_A * (uu * u)))
        hidden[:, columns] = (0.5 * u * (1.0 + t)).astype(BF)
        slope = 0.5 * (1.0 + t) + 0.5 * u * (1.0 - t * t) * (GELU_C * (1.0 + 3.0 * GELU_A * uu))
        pg[:, columns] = (gout[:, columns].astype(F32) * slope).astype(BF)
        return carry

    lax.fori_loop(0, HID // 256, activate, 0)

    acc2[...] = dot(pg[...], right_t[...])
    sa_b[...] = acc2[...].astype(BF)
    ar = AllReduce(acc2, sa_b, sb_b, ra_b, rb_b, back)
    ar.start()

    def term(slot):
        return dot(pg[...], wd_t[slot])

    far = []
    for i in range(MB):
        gsend[12 + i] = term(12 + i).astype(BF)
        for h in range(2):
            rows = pl.ds(h * 128, 128)
            far.append(launch(gsend.at[12 + i, rows], rx.at[12 + i, rows], tensor=s ^ 12))

    def near(level, mask):
        def body(i, carry):
            gsend[MB * level + i] = term(MB * level + i).astype(BF)
            return carry

        lax.fori_loop(0, MB, body, 0)
        view = pl.ds(MB * level, MB)
        return launch(gsend.at[view], rx.at[view], tensor=s ^ mask)

    nears = [near(5, 16), near(2, 2), near(1, 1)]

    def g4_body(i, carry):
        g4[i] = term(9 + i)
        return carry

    lax.fori_loop(0, MB, g4_body, 0)

    def slot_of(p):
        apart = (p // MB) ^ s
        level = jnp.int32(0)
        for n in range(LEVELS - 1):
            level = level + (apart == (1 << n)).astype(jnp.int32) * (n + 1)
        return level * MB + lax.rem(p, MB)

    def blocks(group):
        def body(n, carry):
            j = group * GCOLS + n
            g = pg[:, pl.ds(pl.multiple_of(j * BLOCK, BLOCK), BLOCK)]
            for k in range(NNZ):
                x = (dot(cand_t[slot_of(pat[j, k])], g) * grad_scale).astype(BF)
                row = 0
                while row < BLOCK:
                    at = k * BLOCK + row
                    piece, inner = at // 96, at % 96
                    size = min(96 - inner, BLOCK - row)
                    tb[j, piece // 2, piece % 2, inner : inner + size, :] = x[row : row + size]
                    row += size
            return carry

        lax.fori_loop(0, GCOLS, body, 0)
        view = pl.ds(group * GCOLS, GCOLS)
        return launch(tb.at[view, :, other], tb_rc.at[view], dp=d ^ 1)

    def spread(sent, received):
        return [launch(sent(chip ^ m), received(m), dp=d ^ (2 * m)) for m in CHIP_MASKS]

    def blocks_sum(group, copy):
        copy.wait_recv()

        def body(c, carry):
            for n in range(GCOLS):
                j = group * GCOLS + n
                tb_s[group, c, n] = (tb[j, c, core].astype(F32) + tb_rc[j, c].astype(F32)).astype(BF)
            return carry

        lax.fori_loop(0, CHIPS, body, 0)
        return spread(lambda c: tb_s.at[group, c], lambda m: tb_r.at[group, m])

    def flat_sum(mine, theirs, out, copy, received):
        copy.wait_recv()

        def body(c, carry):
            out[c] = (mine[c, core].astype(F32) + theirs[c].astype(F32)).astype(BF)
            return carry

        lax.fori_loop(0, CHIPS, body, 0)
        return spread(lambda c: out.at[c], lambda m: received.at[m])

    def far_relay(c):
        i, rows = part(c)
        far[c].wait_recv()
        gsend[9 + i, rows] = (g4[i, rows] + rx[12 + i, rows].astype(F32)).astype(BF)
        nears.append(launch(gsend.at[9 + i, rows], rx.at[9 + i, rows], tensor=s ^ 4))

    def flat_parts(out, t):
        for c in range(CHIPS):
            for h in range(2):
                r = (2 * c + h) * 16
                out[c, h] = t[r : r + 16]

    turned(12, 15)
    core0 = blocks(0)
    ar.step(0)
    far_relay(0)
    core1 = blocks(1)
    flat_parts(tr, (dot(codes[...].T, pg[...]) * grad_scale).astype(BF))
    core_r = launch(tr.at[:, other], tr_rc, dp=d ^ 1)
    eight0 = blocks_sum(0, core0)
    far_relay(1)
    ar.step(1)
    eight1 = blocks_sum(1, core1)
    far_relay(2)
    eight_r = flat_sum(tr, tr_rc, tr_s, core_r, tr_r)

    def g0_body(i, carry):
        g0[i] = term(i)
        return carry

    lax.fori_loop(0, MB, g0_body, 0)
    far_relay(3)
    ar.step(2)
    far_relay(4)
    far_relay(5)
    ar.step(3)
    flat_parts(tl, (dot(back[...].T, tokens()) * grad_scale).astype(BF))
    core_l = launch(tl.at[:, other], tl_rc, dp=d ^ 1)
    low = dot(back[...], left_t[...])
    for i in range(MB):
        g0[i] = g0[i] + low[:, i * BLOCK : (i + 1) * BLOCK]
    eight_l = flat_sum(tl, tl_rc, tl_s, core_l, tl_r)

    def sum_flat(own_view, received, copies, out):
        total = own_view[...].astype(F32)
        for m, c in zip(CHIP_MASKS, copies):
            c.wait_recv()
            total = total + received[m].astype(F32)
        out[...] = total

    for group, copies in ((0, eight0), (1, eight1)):
        for c in copies:
            c.wait_recv()

        def body(n, carry, group=group):
            total = tb_s[group, chip, n].astype(F32)
            for m in CHIP_MASKS:
                total = total + tb_r[group, m, n].astype(F32)
            gblk[group * GCOLS + n] = total
            return carry

        lax.fori_loop(0, GCOLS, body, 0)
    sum_flat(tr_s.at[chip], tr_r, eight_r, gright)
    for c in nears:
        c.wait_recv()
    for i in range(MB):
        total = g0[i]
        for level in (1, 2, 3, 5):
            total = total + rx[MB * level + i].astype(F32)
        gtok[:, i * BLOCK : (i + 1) * BLOCK] = total
    sum_flat(tl_s.at[chip], tl_r, eight_l, glt)
    for c in pending:
        c.wait_send()


def per_device(tokens, w_blocks, pattern, low_left, low_right, grad_out):
    grad_scale = 1.0 / math.sqrt(TOK * lax.axis_size("dp"))
    vmem = pl.BlockSpec(memory_space=pltpu.VMEM)
    hbm = pl.BlockSpec(memory_space=pl.ANY)
    V = pltpu.VMEM
    scratch = [
        V((COLS, NNZ, BLOCK, BLOCK), BF), pltpu.SMEM((COLS, NNZ), jnp.int32),
        V((FEAT, RANK), BF), V((RANK, HID), BF), V((TOK, HID), BF), pltpu.SemaphoreType.DMA((8,)),
        V((SLOTS, TOK, BLOCK), BF), V((SLOTS, BLOCK, TOK), BF),
        V((SLOTS, BLOCK, HID), BF), V((SLOTS, HID, BLOCK), BF),
        V((TOK, HID), F32), V((TOK, HID), BF), V((RANK, FEAT), BF), V((HID, RANK), BF),
        V((TOK, RANK), F32), V((TOK, RANK), F32), V((TOK, RANK), BF), V((TOK, RANK), BF),
        V((32, RANK), BF), V((32, RANK), BF), V((7, 32, RANK), BF), V((7, 32, RANK), BF),
        V((3, 16, 128), BF), V((3, 16, 128), BF),
        V((TOK, RANK), BF), V((TOK, RANK), BF),
        V((SLOTS, TOK, BLOCK), BF), V((SLOTS, TOK, BLOCK), BF),
        V((MB, TOK, BLOCK), F32), V((MB, TOK, BLOCK), F32),
        V((COLS, CHIPS, 2, 96, BLOCK), BF), V((COLS, CHIPS, 96, BLOCK), BF),
        V((GROUPS, CHIPS, GCOLS, 96, BLOCK), BF), V((GROUPS, CHIPS, GCOLS, 96, BLOCK), BF),
        V((CHIPS, 2, 16, HID), BF), V((CHIPS, 16, HID), BF), V((CHIPS, 16, HID), BF), V((CHIPS, 16, HID), BF),
        V((CHIPS, 2, 16, FEAT), BF), V((CHIPS, 16, FEAT), BF), V((CHIPS, 16, FEAT), BF), V((CHIPS, 16, FEAT), BF),
        pltpu.SemaphoreType.DMA((NUM_SEMS,)), pltpu.SemaphoreType.DMA((NUM_SEMS,)),
    ]
    out_shape = (
        jax.ShapeDtypeStruct((TOK, HID), BF),
        jax.ShapeDtypeStruct((TOK, FEAT), F32),
        jax.ShapeDtypeStruct((COLS, 96, BLOCK), F32),
        jax.ShapeDtypeStruct((16, FEAT), F32),
        jax.ShapeDtypeStruct((16, HID), F32),
    )
    hidden, gtok, gblk, glt, gright = pl.pallas_call(
        functools.partial(kernel, grad_scale),
        name="pixelfly",
        out_shape=out_shape,
        in_specs=[hbm] * 6,
        out_specs=(vmem,) * 5,
        scratch_shapes=scratch,
        compiler_params=pltpu.CompilerParams(
            collective_id=0, has_side_effects=True, vmem_limit_bytes=56 << 20
        ),
        cost_estimate=pl.CostEstimate(flops=3 << 30, bytes_accessed=6 << 20, transcendentals=TOK * HID),
    )(tokens, w_blocks.reshape(COLS, NNZ, BLOCK, BLOCK), pattern, low_left, low_right, grad_out)
    return hidden, gtok, gblk, glt.T, gright


def solution(mesh):
    in_specs = (
        P("dp", "tensor"),
        P("tensor", None, None),
        P("tensor", None),
        P("tensor", None),
        P(None, "tensor"),
        P("dp", "tensor"),
    )
    out_specs = (
        P("dp", "tensor"),
        P("dp", "tensor"),
        P("tensor", "dp", None),
        P("tensor", "dp"),
        P("dp", "tensor"),
    )
    return jax.shard_map(
        per_device, mesh=mesh, in_specs=in_specs, out_specs=out_specs, check_vma=False
    )
```

```python
import functools
import math

import jax
import jax.numpy as jnp
from jax import lax
from jax.experimental import pallas as pl
from jax.experimental.pallas import tpu as pltpu
from jax.sharding import PartitionSpec as P

MESH = pl.DeviceIdType.MESH
BF, F32 = jnp.bfloat16, jnp.float32
BLOCK = 128
NNZ = 12
TOK = 256
MB = 3
COLS = 6
LEVELS = 6
SLOTS = MB * LEVELS
RANK = 256
HID = COLS * BLOCK
FEAT = MB * BLOCK
GROUPS = 2
GCOLS = COLS // GROUPS
CHIPS = 8
NEAR_GROUP = (19, 18, 17, 16, 3, 2, 1)
FAR_GROUP = (8, 4, 12)
TENSOR_PEERS = tuple(
    near ^ far ^ y for far in (8, 12, 4, 0) for y in (16, 0) for near in (3, 2, 1, 0) if near ^ far ^ y
)
CHIP_MASKS = tuple(range(1, CHIPS))
GELU_C = math.sqrt(2.0 / math.pi)
GELU_A = 0.044715


def dot(a, b):
    return jnp.dot(a, b, preferred_element_type=F32)


class Sems:
    def __init__(self, send, recv):
        self.send, self.recv, self.used = send, recv, 0

    def copy(self, src, dst, **device):
        i = self.used
        self.used += 1
        return pltpu.make_async_remote_copy(
            src_ref=src, dst_ref=dst, send_sem=self.send.at[i], recv_sem=self.recv.at[i],
            device_id=device, device_id_type=MESH,
        )


NUM_SEMS = 160


def kernel(
    grad_scale, tokens_hbm, w_hbm, pat_hbm, left_hbm, right_hbm, gout_hbm,
    hidden, gtok, gblk, glt, gright,
    w, pat, left, right, gout, load_sem,
    cand, cand_t, wd, wd_t, pre, pg, left_t, right_t,
    acc, acc2, sa_f, sa_b, ra_f, ra_b,
    codes, back, gsend, rx, g4, g0,
    tb, tb_rc, tb_s, tb_r, tr, tr_rc, tr_s, tr_r, tl, tl_rc, tl_s, tl_r,
    send_sem, recv_sem,
):
    s = lax.axis_index("tensor")
    d = lax.axis_index("dp")
    core = lax.rem(d, 2)
    chip = d // 2
    other = 1 - core
    sems = Sems(send_sem, recv_sem)
    pending = []

    def launch(src, dst, **device):
        c = sems.copy(src, dst, **device)
        c.start()
        pending.append(c)
        return c

    def fetch(n, src, dst):
        c = pltpu.make_async_copy(src, dst, load_sem.at[n])
        c.start()
        return c

    loads = [fetch(i, tokens_hbm.at[:, pl.ds(i * BLOCK, BLOCK)], cand.at[i]) for i in range(MB)]
    loads.append(fetch(3, left_hbm, left))
    pat_load = fetch(4, pat_hbm, pat)
    w_load = fetch(5, w_hbm, w)
    right_load = fetch(6, right_hbm, right)
    gout_load = fetch(7, gout_hbm, gout)
    barrier = pltpu.get_barrier_semaphore()
    for m in TENSOR_PEERS:
        pl.semaphore_signal(barrier, inc=1, device_id={"tensor": s ^ m}, device_id_type=MESH)
    pl.semaphore_signal(barrier, inc=1, device_id={"dp": d ^ 1}, device_id_type=MESH)
    for m in CHIP_MASKS:
        pl.semaphore_signal(barrier, inc=1, device_id={"dp": d ^ (2 * m)}, device_id_type=MESH)

    for c in loads:
        c.wait()

    def tokens():
        return jnp.concatenate([cand[i] for i in range(MB)], axis=1)

    def in_pieces(out, x):
        for p in range(32):
            row = 32 * ((p & 3) + 4 * (p >> 4)) + 16 * ((p >> 2) & 1)
            column = 128 * ((p >> 3) & 1)
            out[p] = x[row : row + 16, column : column + 128].astype(BF)

    acc[...] = dot(tokens(), left[...])
    in_pieces(sa_f, acc[...])
    pl.semaphore_wait(barrier, len(TENSOR_PEERS) + 1 + len(CHIP_MASKS))

    bit = lambda v, n: lax.rem(lax.shift_right_logical(v, n), 2)
    near_row = pl.multiple_of(32 * (bit(s, 0) + 2 * bit(s, 1) + 4 * bit(s, 4)), 32)
    piece_at = (
        pl.ds(pl.multiple_of(near_row + 16 * bit(s, 2), 16), 16),
        pl.ds(pl.multiple_of(128 * bit(s, 3), 128), 128),
    )

    class AllReduce:
        def __init__(self, total, stage, received, out):
            self.total, self.stage, self.received, self.out = total, stage, received, out

        def start(self):
            self.flying = [
                launch(self.stage.at[s ^ m], self.received.at[n], tensor=s ^ m)
                for n, m in enumerate(TENSOR_PEERS)
            ]

        def step(self, n):
            for c in self.flying:
                c.wait_recv()
            if n == 0:
                part = self.total[piece_at]
                for m in range(len(TENSOR_PEERS)):
                    part = part + self.received[m].astype(F32)
                self.out[piece_at] = part.astype(BF)
                view, group = self.out.at[piece_at], FAR_GROUP
            else:
                view, group = self.out.at[pl.ds(near_row, 32)], NEAR_GROUP
            if n < 2:
                self.flying = [launch(view, view, tensor=s ^ m) for m in group]

    ar = AllReduce(acc, sa_f, ra_f, codes)
    ar.start()

    four = [launch(cand.at[i], cand.at[9 + i], tensor=s ^ 4) for i in range(MB)]
    own = cand.at[pl.ds(0, MB)]
    sixteen = launch(own, cand.at[pl.ds(15, MB)], tensor=s ^ 16)
    two = launch(own, cand.at[pl.ds(6, MB)], tensor=s ^ 2)
    one = launch(own, cand.at[pl.ds(3, MB)], tensor=s ^ 1)
    relayed = []

    def relay(i):
        four[i].wait_recv()
        relayed.append(launch(cand.at[9 + i], cand.at[12 + i], tensor=s ^ 12))

    def dense(first, last):
        def body(slot, carry):
            level = slot // MB
            mask = lax.shift_right_logical(lax.shift_left(jnp.int32(1), level), 1)
            row = (s ^ mask) * MB + lax.rem(slot, MB)
            for j in range(COLS):
                k = jnp.int32(0)
                found = jnp.int32(0)
                for q in range(NNZ):
                    hit = pat[j, q] == row
                    k = jnp.where(hit, q, k)
                    found = jnp.where(hit, 1, found)
                block = jnp.where(found > 0, w[j, k], jnp.zeros((BLOCK, BLOCK), BF))
                wd[slot, :, j * BLOCK : (j + 1) * BLOCK] = block
                wd_t[slot, j * BLOCK : (j + 1) * BLOCK, :] = block.T
            return carry

        lax.fori_loop(first, last, body, 0)

    def turned(first, last):
        def body(slot, carry):
            cand_t[slot] = cand[slot].T
            return carry

        lax.fori_loop(first, last, body, 0)

    def forward(slots, start=None):
        def body(n, carry):
            columns = pl.ds(pl.multiple_of(n * 256, 256), 256)
            total = start(columns) if start is not None else pre[:, columns]
            for p in range(0, len(slots), 2):
                pair = slots[p : p + 2]
                x = jnp.concatenate([cand[q] for q in pair], axis=1)
                y = jnp.concatenate([wd[q, :, columns] for q in pair], axis=0)
                total = total + dot(x, y)
            pre[:, columns] = total
            return carry

        lax.fori_loop(0, HID // 256, body, 0)

    pat_load.wait()
    w_load.wait()
    dense(0, 6)
    relay(0)
    dense(6, 9)
    ar.step(0)
    dense(9, 15)
    relay(1)
    dense(15, 18)
    right_load.wait()
    left_t[...] = left[...].T
    right_t[...] = right[...].T
    turned(0, 3)
    relay(2)
    sixteen.wait_recv()
    turned(15, 18)
    ar.step(1)
    one.wait_recv()
    two.wait_recv()
    turned(3, 9)
    forward((0, 1, 2, 15, 16, 17, 3, 4, 5, 6, 7, 8), lambda columns: jnp.zeros((TOK, 256), F32))
    turned(9, 12)
    forward((9, 10, 11))
    gout_load.wait()
    ar.step(2)
    for c in relayed:
        c.wait_recv()
    def activate(n, carry):
        columns = pl.ds(pl.multiple_of(n * 256, 256), 256)
        u = pre[:, columns]
        u = u + dot(jnp.concatenate([cand[12], cand[13]], axis=1),
                    jnp.concatenate([wd[12, :, columns], wd[13, :, columns]], axis=0))
        u = u + dot(cand[14], wd[14, :, columns])
        u = u + dot(codes[...], right[:, columns])
        uu = u * u
        t = jnp.tanh(GELU_C * (u + GELU_A * (uu * u)))
        hidden[:, columns] = (0.5 * u * (1.0 + t)).astype(BF)
        slope = 0.5 * (1.0 + t) + 0.5 * u * (1.0 - t * t) * (GELU_C * (1.0 + 3.0 * GELU_A * uu))
        pg[:, columns] = (gout[:, columns].astype(F32) * slope).astype(BF)
        return carry

    lax.fori_loop(0, HID // 256, activate, 0)

    acc2[...] = dot(pg[...], right_t[...])
    in_pieces(sa_b, acc2[...])
    ar = AllReduce(acc2, sa_b, ra_b, back)
    ar.start()

    def term(slot):
        return dot(pg[...], wd_t[slot])

    far = []
    for i in range(MB):
        gsend[12 + i] = term(12 + i).astype(BF)
        far.append(launch(gsend.at[12 + i], rx.at[12 + i], tensor=s ^ 12))

    def near(level, mask):
        def body(i, carry):
            gsend[MB * level + i] = term(MB * level + i).astype(BF)
            return carry

        lax.fori_loop(0, MB, body, 0)
        view = pl.ds(MB * level, MB)
        return launch(gsend.at[view], rx.at[view], tensor=s ^ mask)

    nears = [near(5, 16), near(2, 2), near(1, 1)]

    def g4_body(i, carry):
        g4[i] = term(9 + i)
        return carry

    lax.fori_loop(0, MB, g4_body, 0)

    def slot_of(p):
        apart = (p // MB) ^ s
        level = jnp.int32(0)
        for n in range(LEVELS - 1):
            level = level + (apart == (1 << n)).astype(jnp.int32) * (n + 1)
        return level * MB + lax.rem(p, MB)

    def blocks(group):
        def body(n, carry):
            j = group * GCOLS + n
            g = pg[:, pl.ds(pl.multiple_of(j * BLOCK, BLOCK), BLOCK)]
            for k in range(NNZ):
                x = (dot(cand_t[slot_of(pat[j, k])], g) * grad_scale).astype(BF)
                row = 0
                while row < BLOCK:
                    at = k * BLOCK + row
                    piece, inner = at // 96, at % 96
                    size = min(96 - inner, BLOCK - row)
                    tb[j, piece // 2, piece % 2, inner : inner + size, :] = x[row : row + size]
                    row += size
            return carry

        lax.fori_loop(0, GCOLS, body, 0)
        view = pl.ds(group * GCOLS, GCOLS)
        return launch(tb.at[view, :, other], tb_rc.at[view], dp=d ^ 1)

    def spread(sent, received):
        return [launch(sent(chip ^ m), received(m), dp=d ^ (2 * m)) for m in CHIP_MASKS]

    def blocks_sum(group, copy):
        copy.wait_recv()

        def body(c, carry):
            for n in range(GCOLS):
                j = group * GCOLS + n
                tb_s[group, c, n] = (tb[j, c, core].astype(F32) + tb_rc[j, c].astype(F32)).astype(BF)
            return carry

        lax.fori_loop(0, CHIPS, body, 0)
        return spread(lambda c: tb_s.at[group, c], lambda m: tb_r.at[group, m])

    def flat_sum(mine, theirs, out, copy, received):
        copy.wait_recv()

        def body(c, carry):
            out[c] = (mine[c, core].astype(F32) + theirs[c].astype(F32)).astype(BF)
            return carry

        lax.fori_loop(0, CHIPS, body, 0)
        return spread(lambda c: out.at[c], lambda m: received.at[m])

    def far_relay(i):
        far[i].wait_recv()
        gsend[9 + i] = (g4[i] + rx[12 + i].astype(F32)).astype(BF)
        nears.append(launch(gsend.at[9 + i], rx.at[9 + i], tensor=s ^ 4))

    def flat_parts(out, t):
        for c in range(CHIPS):
            for h in range(2):
                r = (2 * c + h) * 16
                out[c, h] = t[r : r + 16]

    turned(12, 15)
    core0 = blocks(0)
    core1 = blocks(1)
    flat_parts(tr, (dot(codes[...].T, pg[...]) * grad_scale).astype(BF))
    core_r = launch(tr.at[:, other], tr_rc, dp=d ^ 1)
    far_relay(0)
    eight0 = blocks_sum(0, core0)
    ar.step(0)
    eight1 = blocks_sum(1, core1)
    far_relay(1)
    eight_r = flat_sum(tr, tr_rc, tr_s, core_r, tr_r)

    def g0_body(i, carry):
        g0[i] = term(i)
        return carry

    lax.fori_loop(0, MB, g0_body, 0)
    far_relay(2)
    ar.step(1)
    ar.step(2)
    flat_parts(tl, (dot(back[...].T, tokens()) * grad_scale).astype(BF))
    core_l = launch(tl.at[:, other], tl_rc, dp=d ^ 1)
    low = dot(back[...], left_t[...])
    for i in range(MB):
        g0[i] = g0[i] + low[:, i * BLOCK : (i + 1) * BLOCK]
    eight_l = flat_sum(tl, tl_rc, tl_s, core_l, tl_r)

    def sum_flat(own_view, received, copies, out):
        total = own_view[...].astype(F32)
        for m, c in zip(CHIP_MASKS, copies):
            c.wait_recv()
            total = total + received[m].astype(F32)
        out[...] = total

    for group, copies in ((0, eight0), (1, eight1)):
        for c in copies:
            c.wait_recv()

        def body(n, carry, group=group):
            total = tb_s[group, chip, n].astype(F32)
            for m in CHIP_MASKS:
                total = total + tb_r[group, m, n].astype(F32)
            gblk[group * GCOLS + n] = total
            return carry

        lax.fori_loop(0, GCOLS, body, 0)
    sum_flat(tr_s.at[chip], tr_r, eight_r, gright)
    for c in nears:
        c.wait_recv()
    for i in range(MB):
        total = g0[i]
        for level in (1, 2, 3, 5):
            total = total + rx[MB * level + i].astype(F32)
        gtok[:, i * BLOCK : (i + 1) * BLOCK] = total
    sum_flat(tl_s.at[chip], tl_r, eight_l, glt)
    for c in pending:
        c.wait_send()


def per_device(tokens, w_blocks, pattern, low_left, low_right, grad_out):
    grad_scale = 1.0 / math.sqrt(TOK * lax.axis_size("dp"))
    vmem = pl.BlockSpec(memory_space=pltpu.VMEM)
    hbm = pl.BlockSpec(memory_space=pltpu.HBM)
    V = pltpu.VMEM
    scratch = [
        V((COLS, NNZ, BLOCK, BLOCK), BF), pltpu.SMEM((COLS, NNZ), jnp.int32),
        V((FEAT, RANK), BF), V((RANK, HID), BF), V((TOK, HID), BF), pltpu.SemaphoreType.DMA((8,)),
        V((SLOTS, TOK, BLOCK), BF), V((SLOTS, BLOCK, TOK), BF),
        V((SLOTS, BLOCK, HID), BF), V((SLOTS, HID, BLOCK), BF),
        V((TOK, HID), F32), V((TOK, HID), BF), V((RANK, FEAT), BF), V((HID, RANK), BF),
        V((TOK, RANK), F32), V((TOK, RANK), F32), V((32, 16, 128), BF), V((32, 16, 128), BF),
        V((31, 16, 128), BF), V((31, 16, 128), BF),
        V((TOK, RANK), BF), V((TOK, RANK), BF),
        V((SLOTS, TOK, BLOCK), BF), V((SLOTS, TOK, BLOCK), BF),
        V((MB, TOK, BLOCK), F32), V((MB, TOK, BLOCK), F32),
        V((COLS, CHIPS, 2, 96, BLOCK), BF), V((COLS, CHIPS, 96, BLOCK), BF),
        V((GROUPS, CHIPS, GCOLS, 96, BLOCK), BF), V((GROUPS, CHIPS, GCOLS, 96, BLOCK), BF),
        V((CHIPS, 2, 16, HID), BF), V((CHIPS, 16, HID), BF), V((CHIPS, 16, HID), BF), V((CHIPS, 16, HID), BF),
        V((CHIPS, 2, 16, FEAT), BF), V((CHIPS, 16, FEAT), BF), V((CHIPS, 16, FEAT), BF), V((CHIPS, 16, FEAT), BF),
        pltpu.SemaphoreType.DMA((NUM_SEMS,)), pltpu.SemaphoreType.DMA((NUM_SEMS,)),
    ]
    out_shape = (
        V((TOK, HID), BF),
        V((TOK, FEAT), F32),
        V((COLS, 96, BLOCK), F32),
        V((16, FEAT), F32),
        V((16, HID), F32),
    )
    hidden, gtok, gblk, glt, gright = pl.pallas_call(
        functools.partial(kernel, grad_scale),
        name="pixelfly",
        out_shape=out_shape,
        in_specs=[hbm] * 6,
        out_specs=(vmem,) * 5,
        scratch_shapes=scratch,
        compiler_params=pltpu.CompilerParams(
            collective_id=0, has_side_effects=True, vmem_limit_bytes=56 << 20
        ),
        cost_estimate=pl.CostEstimate(flops=3 << 30, bytes_accessed=6 << 20, transcendentals=TOK * HID),
    )(tokens, w_blocks.reshape(COLS, NNZ, BLOCK, BLOCK), pattern, low_left, low_right, grad_out)
    return hidden, gtok, gblk, glt.T, gright


def solution(mesh):
    in_specs = (
        P("dp", "tensor"),
        P("tensor", None, None),
        P("tensor", None),
        P("tensor", None),
        P(None, "tensor"),
        P("dp", "tensor"),
    )
    out_specs = (
        P("dp", "tensor"),
        P("dp", "tensor"),
        P("tensor", "dp", None),
        P("tensor", "dp"),
        P("dp", "tensor"),
    )
    return jax.shard_map(
        per_device, mesh=mesh, in_specs=in_specs, out_specs=out_specs, check_vma=False
    )
```

```python
import functools
import math

import jax
import jax.numpy as jnp
from jax import lax
from jax.experimental import pallas as pl
from jax.experimental.pallas import tpu as pltpu
from jax.sharding import PartitionSpec as P

MESH = pl.DeviceIdType.MESH
BF, F32 = jnp.bfloat16, jnp.float32
BLOCK = 128
NNZ = 12
TOK = 256
MB = 3
COLS = 6
LEVELS = 6
SLOTS = MB * LEVELS
RANK = 256
HID = COLS * BLOCK
FEAT = MB * BLOCK
GROUPS = 2
GCOLS = COLS // GROUPS
CHIPS = 8
NEAR_GROUP = (19, 18, 17, 16, 3, 2, 1)
FAR_GROUP = (8, 4, 12)
TENSOR_PEERS = tuple(
    near ^ far ^ y for far in (8, 12, 4, 0) for y in (16, 0) for near in (3, 2, 1, 0) if near ^ far ^ y
)
CHIP_MASKS = tuple(range(1, CHIPS))
GELU_C = math.sqrt(2.0 / math.pi)
GELU_A = 0.044715


def dot(a, b):
    return jnp.dot(a, b, preferred_element_type=F32)


class Sems:
    def __init__(self, send, recv):
        self.send, self.recv, self.used = send, recv, 0

    def copy(self, src, dst, **device):
        i = self.used
        self.used += 1
        return pltpu.make_async_remote_copy(
            src_ref=src, dst_ref=dst, send_sem=self.send.at[i], recv_sem=self.recv.at[i],
            device_id=device, device_id_type=MESH,
        )


NUM_SEMS = 160


def kernel(
    grad_scale, tokens_hbm, w_hbm, pat_hbm, left_hbm, right_hbm, gout_hbm,
    hidden, gtok, gblk, glt, gright,
    w, pat, left, right, gout, load_sem,
    cand, cand_t, wd, wd_t, pre, pg, left_t, right_t,
    acc, acc2, sa_f, sb_f, ra_f, rb_f, sa_b, ra_b,
    codes, back, gsend, rx, g4, g0,
    tb, tb_rc, tb_s, tb_r, tr, tr_rc, tr_s, tr_r, tl, tl_rc, tl_s, tl_r,
    send_sem, recv_sem,
):
    s = lax.axis_index("tensor")
    d = lax.axis_index("dp")
    core = lax.rem(d, 2)
    chip = d // 2
    other = 1 - core
    sems = Sems(send_sem, recv_sem)
    pending = []

    def launch(src, dst, **device):
        c = sems.copy(src, dst, **device)
        c.start()
        pending.append(c)
        return c

    barrier = pltpu.get_barrier_semaphore()
    for m in TENSOR_PEERS:
        pl.semaphore_signal(barrier, inc=1, device_id={"tensor": s ^ m}, device_id_type=MESH)
    pl.semaphore_signal(barrier, inc=1, device_id={"dp": d ^ 1}, device_id_type=MESH)
    for m in CHIP_MASKS:
        pl.semaphore_signal(barrier, inc=1, device_id={"dp": d ^ (2 * m)}, device_id_type=MESH)

    def fetch(n, src, dst):
        c = pltpu.make_async_copy(src, dst, load_sem.at[n])
        c.start()
        return c

    loads = [fetch(i, tokens_hbm.at[:, pl.ds(i * BLOCK, BLOCK)], cand.at[i]) for i in range(MB)]
    loads.append(fetch(3, left_hbm, left))
    pat_load = fetch(4, pat_hbm, pat)
    w_load = fetch(5, w_hbm, w)
    right_load = fetch(6, right_hbm, right)
    gout_load = fetch(7, gout_hbm, gout)
    for c in loads:
        c.wait()

    def tokens():
        return jnp.concatenate([cand[i] for i in range(MB)], axis=1)

    def in_pieces(out, x):
        for p in range(32):
            row = 32 * ((p & 3) + 4 * (p >> 4)) + 16 * ((p >> 2) & 1)
            column = 128 * ((p >> 3) & 1)
            out[p] = x[row : row + 16, column : column + 128].astype(BF)

    acc[...] = dot(tokens(), left[...])
    sa_f[...] = acc[...].astype(BF)
    pl.semaphore_wait(barrier, len(TENSOR_PEERS) + 1 + len(CHIP_MASKS))

    bit = lambda v, n: lax.rem(lax.shift_right_logical(v, n), 2)
    near_row = pl.multiple_of(32 * (bit(s, 0) + 2 * bit(s, 1) + 4 * bit(s, 4)), 32)
    piece_at = (
        pl.ds(pl.multiple_of(near_row + 16 * bit(s, 2), 16), 16),
        pl.ds(pl.multiple_of(128 * bit(s, 3), 128), 128),
    )

    class AllReduce:
        def __init__(self, total, stage, received, out):
            self.total, self.stage, self.received, self.out = total, stage, received, out

        def start(self):
            self.flying = [
                launch(self.stage.at[s ^ m], self.received.at[n], tensor=s ^ m)
                for n, m in enumerate(TENSOR_PEERS)
            ]

        def step(self, n):
            for c in self.flying:
                c.wait_recv()
            if n == 0:
                part = self.total[piece_at]
                for m in range(len(TENSOR_PEERS)):
                    part = part + self.received[m].astype(F32)
                self.out[piece_at] = part.astype(BF)
                view, group = self.out.at[piece_at], FAR_GROUP
            else:
                view, group = self.out.at[pl.ds(near_row, 32)], NEAR_GROUP
            if n < 2:
                self.flying = [launch(view, view, tensor=s ^ m) for m in group]

    class NearFirst:
        def __init__(self, total, near_stage, near_in, far_stage, far_in, out):
            self.total, self.near_stage, self.near_in = total, near_stage, near_in
            self.far_stage, self.far_in, self.out = far_stage, far_in, out

        def start(self):
            def row(v):
                return pl.multiple_of(32 * (bit(v, 0) + 2 * bit(v, 1) + 4 * bit(v, 4)), 32)

            self.flying = [
                launch(self.near_stage.at[pl.ds(row(s ^ m), 32)], self.near_in.at[n], tensor=s ^ m)
                for n, m in enumerate(NEAR_GROUP)
            ]

        def step(self, n):
            for c in self.flying:
                c.wait_recv()
            rows, piece = pl.ds(near_row, 32), self.out.at[piece_at]
            if n == 0:
                part = self.total[rows, :]
                for m in range(len(NEAR_GROUP)):
                    part = part + self.near_in[m].astype(F32)
                self.total[rows, :] = part
                self.far_stage[...] = part.astype(BF)
                self.flying = []
                for i, m in enumerate(FAR_GROUP):
                    at = (
                        pl.ds(pl.multiple_of(16 * bit(s ^ m, 2), 16), 16),
                        pl.ds(pl.multiple_of(128 * bit(s ^ m, 3), 128), 128),
                    )
                    self.flying.append(launch(self.far_stage.at[at], self.far_in.at[i], tensor=s ^ m))
            elif n == 1:
                part = self.total[piece_at]
                for m in range(len(FAR_GROUP)):
                    part = part + self.far_in[m].astype(F32)
                piece[...] = part.astype(BF)
                self.flying = [launch(piece, piece, tensor=s ^ m) for m in FAR_GROUP]
            elif n == 2:
                view = self.out.at[rows]
                self.flying = [launch(view, view, tensor=s ^ m) for m in NEAR_GROUP]

    four, relayed = [], []

    def part(c):
        return c // 2, pl.ds((c % 2) * 128, 128)

    def send_four(first, last):
        for c in range(first, last):
            i, rows = part(c)
            four.append(launch(cand.at[i, rows], cand.at[9 + i, rows], tensor=s ^ 4))

    def relay(c):
        i, rows = part(c)
        four[c].wait_recv()
        relayed.append(launch(cand.at[9 + i, rows], cand.at[12 + i, rows], tensor=s ^ 12))

    ar = NearFirst(acc, sa_f, ra_f, sb_f, rb_f, codes)
    send_four(0, 2)
    ar.start()
    send_four(2, 6)
    own = cand.at[pl.ds(0, MB)]
    sixteen = launch(own, cand.at[pl.ds(15, MB)], tensor=s ^ 16)
    two = launch(own, cand.at[pl.ds(6, MB)], tensor=s ^ 2)
    one = launch(own, cand.at[pl.ds(3, MB)], tensor=s ^ 1)

    def dense(first, last):
        def body(slot, carry):
            level = slot // MB
            mask = lax.shift_right_logical(lax.shift_left(jnp.int32(1), level), 1)
            row = (s ^ mask) * MB + lax.rem(slot, MB)
            for j in range(COLS):
                k = jnp.int32(0)
                found = jnp.int32(0)
                for q in range(NNZ):
                    hit = pat[j, q] == row
                    k = jnp.where(hit, q, k)
                    found = jnp.where(hit, 1, found)
                block = jnp.where(found > 0, w[j, k], jnp.zeros((BLOCK, BLOCK), BF))
                wd[slot, :, j * BLOCK : (j + 1) * BLOCK] = block
                wd_t[slot, j * BLOCK : (j + 1) * BLOCK, :] = block.T
            return carry

        lax.fori_loop(first, last, body, 0)

    def turned(first, last):
        def body(slot, carry):
            cand_t[slot] = cand[slot].T
            return carry

        lax.fori_loop(first, last, body, 0)

    def forward(slots, start=None):
        def body(n, carry):
            columns = pl.ds(pl.multiple_of(n * 256, 256), 256)
            total = start(columns) if start is not None else pre[:, columns]
            for p in range(0, len(slots), 2):
                pair = slots[p : p + 2]
                x = jnp.concatenate([cand[q] for q in pair], axis=1)
                y = jnp.concatenate([wd[q, :, columns] for q in pair], axis=0)
                total = total + dot(x, y)
            pre[:, columns] = total
            return carry

        lax.fori_loop(0, HID // 256, body, 0)

    pat_load.wait()
    w_load.wait()
    dense(0, 4)
    relay(0)
    ar.step(0)
    dense(4, 8)
    relay(1)
    dense(8, 12)
    relay(2)
    ar.step(1)
    dense(12, 15)
    relay(3)
    dense(15, 18)
    right_load.wait()
    left_t[...] = left[...].T
    relay(4)
    right_t[...] = right[...].T
    turned(0, 3)
    sixteen.wait_recv()
    turned(15, 18)
    relay(5)
    ar.step(2)
    one.wait_recv()
    two.wait_recv()
    turned(3, 9)
    forward((0, 1, 2, 15, 16, 17, 3, 4, 5, 6, 7, 8), lambda columns: jnp.zeros((TOK, 256), F32))
    turned(9, 12)
    forward((9, 10, 11))
    gout_load.wait()
    ar.step(3)
    for c in relayed:
        c.wait_recv()
    def activate(n, carry):
        columns = pl.ds(pl.multiple_of(n * 256, 256), 256)
        u = pre[:, columns]
        u = u + dot(jnp.concatenate([cand[12], cand[13]], axis=1),
                    jnp.concatenate([wd[12, :, columns], wd[13, :, columns]], axis=0))
        u = u + dot(cand[14], wd[14, :, columns])
        u = u + dot(codes[...], right[:, columns])
        uu = u * u
        t = jnp.tanh(GELU_C * (u + GELU_A * (uu * u)))
        hidden[:, columns] = (0.5 * u * (1.0 + t)).astype(BF)
        slope = 0.5 * (1.0 + t) + 0.5 * u * (1.0 - t * t) * (GELU_C * (1.0 + 3.0 * GELU_A * uu))
        pg[:, columns] = (gout[:, columns].astype(F32) * slope).astype(BF)
        return carry

    lax.fori_loop(0, HID // 256, activate, 0)

    acc2[...] = dot(pg[...], right_t[...])
    in_pieces(sa_b, acc2[...])
    ar = AllReduce(acc2, sa_b, ra_b, back)
    ar.start()

    def term(slot):
        return dot(pg[...], wd_t[slot])

    far = []
    for i in range(MB):
        gsend[12 + i] = term(12 + i).astype(BF)
        far.append(launch(gsend.at[12 + i], rx.at[12 + i], tensor=s ^ 12))

    def near(level, mask):
        def body(i, carry):
            gsend[MB * level + i] = term(MB * level + i).astype(BF)
            return carry

        lax.fori_loop(0, MB, body, 0)
        view = pl.ds(MB * level, MB)
        return launch(gsend.at[view], rx.at[view], tensor=s ^ mask)

    nears = [near(5, 16), near(2, 2), near(1, 1)]

    def g4_body(i, carry):
        g4[i] = term(9 + i)
        return carry

    lax.fori_loop(0, MB, g4_body, 0)

    def slot_of(p):
        apart = (p // MB) ^ s
        level = jnp.int32(0)
        for n in range(LEVELS - 1):
            level = level + (apart == (1 << n)).astype(jnp.int32) * (n + 1)
        return level * MB + lax.rem(p, MB)

    def blocks(group):
        def body(n, carry):
            j = group * GCOLS + n
            g = pg[:, pl.ds(pl.multiple_of(j * BLOCK, BLOCK), BLOCK)]
            for k in range(NNZ):
                x = (dot(cand_t[slot_of(pat[j, k])], g) * grad_scale).astype(BF)
                row = 0
                while row < BLOCK:
                    at = k * BLOCK + row
                    piece, inner = at // 96, at % 96
                    size = min(96 - inner, BLOCK - row)
                    tb[j, piece // 2, piece % 2, inner : inner + size, :] = x[row : row + size]
                    row += size
            return carry

        lax.fori_loop(0, GCOLS, body, 0)
        view = pl.ds(group * GCOLS, GCOLS)
        return launch(tb.at[view, :, other], tb_rc.at[view], dp=d ^ 1)

    def spread(sent, received):
        return [launch(sent(chip ^ m), received(m), dp=d ^ (2 * m)) for m in CHIP_MASKS]

    def blocks_sum(group, copy):
        copy.wait_recv()

        def body(c, carry):
            for n in range(GCOLS):
                j = group * GCOLS + n
                tb_s[group, c, n] = (tb[j, c, core].astype(F32) + tb_rc[j, c].astype(F32)).astype(BF)
            return carry

        lax.fori_loop(0, CHIPS, body, 0)
        return spread(lambda c: tb_s.at[group, c], lambda m: tb_r.at[group, m])

    def flat_sum(mine, theirs, out, copy, received):
        copy.wait_recv()

        def body(c, carry):
            out[c] = (mine[c, core].astype(F32) + theirs[c].astype(F32)).astype(BF)
            return carry

        lax.fori_loop(0, CHIPS, body, 0)
        return spread(lambda c: out.at[c], lambda m: received.at[m])

    def far_relay(i):
        far[i].wait_recv()
        gsend[9 + i] = (g4[i] + rx[12 + i].astype(F32)).astype(BF)
        nears.append(launch(gsend.at[9 + i], rx.at[9 + i], tensor=s ^ 4))

    def flat_parts(out, t):
        for c in range(CHIPS):
            for h in range(2):
                r = (2 * c + h) * 16
                out[c, h] = t[r : r + 16]

    turned(12, 15)
    core0 = blocks(0)
    core1 = blocks(1)
    flat_parts(tr, (dot(codes[...].T, pg[...]) * grad_scale).astype(BF))
    core_r = launch(tr.at[:, other], tr_rc, dp=d ^ 1)
    far_relay(0)
    eight0 = blocks_sum(0, core0)
    ar.step(0)
    eight1 = blocks_sum(1, core1)
    far_relay(1)
    eight_r = flat_sum(tr, tr_rc, tr_s, core_r, tr_r)

    def g0_body(i, carry):
        g0[i] = term(i)
        return carry

    lax.fori_loop(0, MB, g0_body, 0)
    far_relay(2)
    ar.step(1)
    ar.step(2)
    flat_parts(tl, (dot(back[...].T, tokens()) * grad_scale).astype(BF))
    core_l = launch(tl.at[:, other], tl_rc, dp=d ^ 1)
    low = dot(back[...], left_t[...])
    for i in range(MB):
        g0[i] = g0[i] + low[:, i * BLOCK : (i + 1) * BLOCK]
    eight_l = flat_sum(tl, tl_rc, tl_s, core_l, tl_r)

    def sum_flat(own_view, received, copies, out):
        total = own_view[...].astype(F32)
        for m, c in zip(CHIP_MASKS, copies):
            c.wait_recv()
            total = total + received[m].astype(F32)
        out[...] = total

    for group, copies in ((0, eight0), (1, eight1)):
        for c in copies:
            c.wait_recv()

        def body(n, carry, group=group):
            total = tb_s[group, chip, n].astype(F32)
            for m in CHIP_MASKS:
                total = total + tb_r[group, m, n].astype(F32)
            gblk[group * GCOLS + n] = total
            return carry

        lax.fori_loop(0, GCOLS, body, 0)
    sum_flat(tr_s.at[chip], tr_r, eight_r, gright)
    for c in nears:
        c.wait_recv()
    for i in range(MB):
        total = g0[i]
        for level in (1, 2, 3, 5):
            total = total + rx[MB * level + i].astype(F32)
        gtok[:, i * BLOCK : (i + 1) * BLOCK] = total
    sum_flat(tl_s.at[chip], tl_r, eight_l, glt)
    for c in pending:
        c.wait_send()


def hand_over(*refs):
    n = len(refs) // 2
    copies = [pltpu.make_async_copy(refs[i], refs[n + i], refs[-1].at[i]) for i in range(n)]
    for c in copies:
        c.start()
    for c in copies:
        c.wait()


def per_device(tokens, w_blocks, pattern, low_left, low_right, grad_out):
    grad_scale = 1.0 / math.sqrt(TOK * lax.axis_size("dp"))
    vmem = pl.BlockSpec(memory_space=pltpu.VMEM)
    hbm = pl.BlockSpec(memory_space=pltpu.HBM)
    V = pltpu.VMEM
    scratch = [
        V((COLS, NNZ, BLOCK, BLOCK), BF), pltpu.SMEM((COLS, NNZ), jnp.int32),
        V((FEAT, RANK), BF), V((RANK, HID), BF), V((TOK, HID), BF), pltpu.SemaphoreType.DMA((8,)),
        V((SLOTS, TOK, BLOCK), BF), V((SLOTS, BLOCK, TOK), BF),
        V((SLOTS, BLOCK, HID), BF), V((SLOTS, HID, BLOCK), BF),
        V((TOK, HID), F32), V((TOK, HID), BF), V((RANK, FEAT), BF), V((HID, RANK), BF),
        V((TOK, RANK), F32), V((TOK, RANK), F32), V((TOK, RANK), BF), V((32, RANK), BF),
        V((7, 32, RANK), BF), V((3, 16, 128), BF), V((32, 16, 128), BF), V((31, 16, 128), BF),
        V((TOK, RANK), BF), V((TOK, RANK), BF),
        V((SLOTS, TOK, BLOCK), BF), V((SLOTS, TOK, BLOCK), BF),
        V((MB, TOK, BLOCK), F32), V((MB, TOK, BLOCK), F32),
        V((COLS, CHIPS, 2, 96, BLOCK), BF), V((COLS, CHIPS, 96, BLOCK), BF),
        V((GROUPS, CHIPS, GCOLS, 96, BLOCK), BF), V((GROUPS, CHIPS, GCOLS, 96, BLOCK), BF),
        V((CHIPS, 2, 16, HID), BF), V((CHIPS, 16, HID), BF), V((CHIPS, 16, HID), BF), V((CHIPS, 16, HID), BF),
        V((CHIPS, 2, 16, FEAT), BF), V((CHIPS, 16, FEAT), BF), V((CHIPS, 16, FEAT), BF), V((CHIPS, 16, FEAT), BF),
        pltpu.SemaphoreType.DMA((NUM_SEMS,)), pltpu.SemaphoreType.DMA((NUM_SEMS,)),
    ]
    out_shape = (
        V((TOK, HID), BF),
        V((TOK, FEAT), F32),
        V((COLS, 96, BLOCK), F32),
        V((16, FEAT), F32),
        V((16, HID), F32),
    )
    results = pl.pallas_call(
        functools.partial(kernel, grad_scale),
        name="pixelfly",
        out_shape=out_shape,
        in_specs=[hbm] * 6,
        out_specs=(vmem,) * 5,
        scratch_shapes=scratch,
        compiler_params=pltpu.CompilerParams(
            collective_id=0, has_side_effects=True, vmem_limit_bytes=56 << 20
        ),
        cost_estimate=pl.CostEstimate(flops=3 << 30, bytes_accessed=6 << 20, transcendentals=TOK * HID),
    )(tokens, w_blocks.reshape(COLS, NNZ, BLOCK, BLOCK), pattern, low_left, low_right, grad_out)
    hidden, gtok, gblk, glt, gright = pl.pallas_call(
        hand_over,
        name="hand_over",
        out_shape=[jax.ShapeDtypeStruct(r.shape, r.dtype) for r in results],
        in_specs=[vmem] * len(results),
        out_specs=[pl.BlockSpec(memory_space=pl.ANY)] * len(results),
        scratch_shapes=[pltpu.SemaphoreType.DMA((len(results),))],
    )(*results)
    return hidden, gtok, gblk, glt.T, gright


def solution(mesh):
    in_specs = (
        P("dp", "tensor"),
        P("tensor", None, None),
        P("tensor", None),
        P("tensor", None),
        P(None, "tensor"),
        P("dp", "tensor"),
    )
    out_specs = (
        P("dp", "tensor"),
        P("dp", "tensor"),
        P("tensor", "dp", None),
        P("tensor", "dp"),
        P("dp", "tensor"),
    )
    return jax.shard_map(
        per_device, mesh=mesh, in_specs=in_specs, out_specs=out_specs, check_vma=False
    )
```

```python
import functools
import math

import jax
import jax.numpy as jnp
from jax import lax
from jax.experimental import pallas as pl
from jax.experimental.pallas import tpu as pltpu
from jax.sharding import PartitionSpec as P

MESH = pl.DeviceIdType.MESH
BF, F32 = jnp.bfloat16, jnp.float32
BLOCK = 128
NNZ = 12
TOK = 256
MB = 3
COLS = 6
LEVELS = 6
SLOTS = MB * LEVELS
RANK = 256
HID = COLS * BLOCK
FEAT = MB * BLOCK
CHUNKS = 6
GROUPS = 2
GCOLS = COLS // GROUPS
CHIPS = 8
NEAR_GROUP = (19, 18, 17, 16, 3, 2, 1)
FAR_GROUP = (8, 4, 12)
TENSOR_PEERS = FAR_GROUP + NEAR_GROUP
CHIP_MASKS = tuple(range(1, CHIPS))
GELU_C = math.sqrt(2.0 / math.pi)
GELU_A = 0.044715


def dot(a, b):
    return jnp.dot(a, b, preferred_element_type=F32)


class Sems:
    def __init__(self, send, recv):
        self.send, self.recv, self.used = send, recv, 0

    def copy(self, src, dst, **device):
        i = self.used
        self.used += 1
        return pltpu.make_async_remote_copy(
            src_ref=src, dst_ref=dst, send_sem=self.send.at[i], recv_sem=self.recv.at[i],
            device_id=device, device_id_type=MESH,
        )


NUM_SEMS = 160


def kernel(
    grad_scale, tokens_hbm, w_hbm, pat_hbm, left_hbm, right_hbm, gout_hbm,
    hidden, gtok, gblk, glt, gright,
    w, pat, left, right, gout, load_sem,
    cand, cand_t, wd, wd_t, pre, pg, left_t, right_t,
    acc, acc2, sa_f, sa_b, sb_f, sb_b, ra_f, ra_b, rb_f, rb_b,
    codes, back, gsend, rx, g4, g0,
    tb, tb_rc, tb_s, tb_r, tr, tr_rc, tr_s, tr_r, tl, tl_rc, tl_s, tl_r,
    send_sem, recv_sem,
):
    s = lax.axis_index("tensor")
    d = lax.axis_index("dp")
    core = lax.rem(d, 2)
    chip = d // 2
    other = 1 - core
    sems = Sems(send_sem, recv_sem)
    pending = []

    def launch(src, dst, **device):
        c = sems.copy(src, dst, **device)
        c.start()
        pending.append(c)
        return c

    barrier = pltpu.get_barrier_semaphore()
    for m in TENSOR_PEERS:
        pl.semaphore_signal(barrier, inc=1, device_id={"tensor": s ^ m}, device_id_type=MESH)
    pl.semaphore_signal(barrier, inc=1, device_id={"dp": d ^ 1}, device_id_type=MESH)
    for m in CHIP_MASKS:
        pl.semaphore_signal(barrier, inc=1, device_id={"dp": d ^ (2 * m)}, device_id_type=MESH)

    def fetch(n, src, dst):
        c = pltpu.make_async_copy(src, dst, load_sem.at[n])
        c.start()
        return c

    loads = [fetch(i, tokens_hbm.at[:, pl.ds(i * BLOCK, BLOCK)], cand.at[i]) for i in range(MB)]
    loads.append(fetch(3, left_hbm, left))
    pat_load = fetch(4, pat_hbm, pat)
    w_load = fetch(5, w_hbm, w)
    right_load = fetch(6, right_hbm, right)
    gout_load = fetch(7, gout_hbm, gout)
    for c in loads:
        c.wait()

    def tokens():
        return jnp.concatenate([cand[i] for i in range(MB)], axis=1)

    acc[...] = dot(tokens(), left[...])
    sa_f[...] = acc[...].astype(BF)
    pl.semaphore_wait(barrier, len(TENSOR_PEERS) + 1 + len(CHIP_MASKS))

    def part(c):
        i, h = c // 2, c % 2
        return i, pl.ds(h * 128, 128)

    bit = lambda v, n: lax.rem(lax.shift_right_logical(v, n), 2)
    near_row = lambda v: pl.multiple_of(32 * (bit(v, 0) + 2 * bit(v, 1) + 4 * bit(v, 4)), 32)
    far_row = lambda v: pl.multiple_of(16 * bit(v, 2), 16)
    far_col = lambda v: pl.multiple_of(128 * bit(v, 3), 128)

    class AllReduce:
        def __init__(self, total, near_stage, far_stage, near_in, far_in, out):
            self.total, self.near_stage, self.far_stage = total, near_stage, far_stage
            self.near_in, self.far_in, self.out = near_in, far_in, out

        def start(self):
            self.flying = [
                launch(self.near_stage.at[pl.ds(near_row(s ^ m), 32)], self.near_in.at[n], tensor=s ^ m)
                for n, m in enumerate(NEAR_GROUP)
            ]

        def arrived(self):
            for c in self.flying:
                c.wait_recv()

        def step(self, n):
            self.arrived()
            rows = pl.ds(near_row(s), 32)
            piece = self.out.at[pl.ds(pl.multiple_of(near_row(s) + far_row(s), 16), 16), pl.ds(far_col(s), 128)]
            if n == 0:
                part = self.total[rows, :]
                for m in range(len(NEAR_GROUP)):
                    part = part + self.near_in[m].astype(F32)
                self.total[rows, :] = part
                self.far_stage[...] = part.astype(BF)
                self.flying = [
                    launch(
                        self.far_stage.at[pl.ds(far_row(s ^ m), 16), pl.ds(far_col(s ^ m), 128)],
                        self.far_in.at[i], tensor=s ^ m,
                    )
                    for i, m in enumerate(FAR_GROUP)
                ]
            elif n == 1:
                part = self.total[
                    pl.ds(pl.multiple_of(near_row(s) + far_row(s), 16), 16), pl.ds(far_col(s), 128)
                ]
                for m in range(len(FAR_GROUP)):
                    part = part + self.far_in[m].astype(F32)
                piece[...] = part.astype(BF)
                self.flying = [launch(piece, piece, tensor=s ^ m) for m in FAR_GROUP]
            elif n == 2:
                view = self.out.at[rows]
                self.flying = [launch(view, view, tensor=s ^ m) for m in NEAR_GROUP]

    four = []
    for c in range(2):
        i, rows = part(c)
        four.append(launch(cand.at[i, rows], cand.at[9 + i, rows], tensor=s ^ 4))
    ar = AllReduce(acc, sa_f, sb_f, ra_f, rb_f, codes)
    ar.start()
    for c in range(2, CHUNKS):
        i, rows = part(c)
        four.append(launch(cand.at[i, rows], cand.at[9 + i, rows], tensor=s ^ 4))
    own = cand.at[pl.ds(0, MB)]
    sixteen = launch(own, cand.at[pl.ds(15, MB)], tensor=s ^ 16)
    two = launch(own, cand.at[pl.ds(6, MB)], tensor=s ^ 2)
    one = launch(own, cand.at[pl.ds(3, MB)], tensor=s ^ 1)
    relayed = []

    def relay(c):
        i, rows = part(c)
        four[c].wait_recv()
        relayed.append(launch(cand.at[9 + i, rows], cand.at[12 + i, rows], tensor=s ^ 12))

    def dense(first, last):
        def body(slot, carry):
            level = slot // MB
            mask = lax.shift_right_logical(lax.shift_left(jnp.int32(1), level), 1)
            row = (s ^ mask) * MB + lax.rem(slot, MB)
            for j in range(COLS):
                k = jnp.int32(0)
                found = jnp.int32(0)
                for q in range(NNZ):
                    hit = pat[j, q] == row
                    k = jnp.where(hit, q, k)
                    found = jnp.where(hit, 1, found)
                block = jnp.where(found > 0, w[j, k], jnp.zeros((BLOCK, BLOCK), BF))
                wd[slot, :, j * BLOCK : (j + 1) * BLOCK] = block
                wd_t[slot, j * BLOCK : (j + 1) * BLOCK, :] = block.T
            return carry

        lax.fori_loop(first, last, body, 0)

    def turned(first, last):
        def body(slot, carry):
            cand_t[slot] = cand[slot].T
            return carry

        lax.fori_loop(first, last, body, 0)

    def forward(slots, start=None):
        def body(n, carry):
            columns = pl.ds(pl.multiple_of(n * 256, 256), 256)
            total = start(columns) if start is not None else pre[:, columns]
            for p in range(0, len(slots), 2):
                pair = slots[p : p + 2]
                x = jnp.concatenate([cand[q] for q in pair], axis=1)
                y = jnp.concatenate([wd[q, :, columns] for q in pair], axis=0)
                total = total + dot(x, y)
            pre[:, columns] = total
            return carry

        lax.fori_loop(0, HID // 256, body, 0)

    pat_load.wait()
    w_load.wait()
    dense(0, 4)
    relay(0)
    ar.step(0)
    dense(4, 8)
    relay(1)
    dense(8, 12)
    relay(2)
    ar.step(1)
    dense(12, 15)
    relay(3)
    dense(15, 18)
    right_load.wait()
    left_t[...] = left[...].T
    relay(4)
    right_t[...] = right[...].T
    turned(0, 3)
    sixteen.wait_recv()
    turned(15, 18)
    relay(5)
    ar.step(2)
    one.wait_recv()
    two.wait_recv()
    turned(3, 9)
    forward((0, 1, 2, 15, 16, 17, 3, 4, 5, 6, 7, 8), lambda columns: jnp.zeros((TOK, 256), F32))
    turned(9, 12)
    forward((9, 10, 11))
    ar.step(3)
    gout_load.wait()
    for c in range(CHUNKS):
        relayed[c].wait_recv()
    def activate(n, carry):
        columns = pl.ds(pl.multiple_of(n * 256, 256), 256)
        u = pre[:, columns]
        u = u + dot(jnp.concatenate([cand[12], cand[13]], axis=1),
                    jnp.concatenate([wd[12, :, columns], wd[13, :, columns]], axis=0))
        u = u + dot(cand[14], wd[14, :, columns])
        u = u + dot(codes[...], right[:, columns])
        uu = u * u
        t = jnp.tanh(GELU_C * (u + GELU_A * (uu * u)))
        hidden[:, columns] = (0.5 * u * (1.0 + t)).astype(BF)
        slope = 0.5 * (1.0 + t) + 0.5 * u * (1.0 - t * t) * (GELU_C * (1.0 + 3.0 * GELU_A * uu))
        pg[:, columns] = (gout[:, columns].astype(F32) * slope).astype(BF)
        return carry

    lax.fori_loop(0, HID // 256, activate, 0)

    acc2[...] = dot(pg[...], right_t[...])
    sa_b[...] = acc2[...].astype(BF)
    ar = AllReduce(acc2, sa_b, sb_b, ra_b, rb_b, back)
    ar.start()

    def term(slot):
        return dot(pg[...], wd_t[slot])

    far = []
    for i in range(MB):
        gsend[12 + i] = term(12 + i).astype(BF)
        for h in range(2):
            rows = pl.ds(h * 128, 128)
            far.append(launch(gsend.at[12 + i, rows], rx.at[12 + i, rows], tensor=s ^ 12))

    def near(level, mask):
        def body(i, carry):
            gsend[MB * level + i] = term(MB * level + i).astype(BF)
            return carry

        lax.fori_loop(0, MB, body, 0)
        view = pl.ds(MB * level, MB)
        return launch(gsend.at[view], rx.at[view], tensor=s ^ mask)

    nears = [near(5, 16), near(2, 2), near(1, 1)]

    def g4_body(i, carry):
        g4[i] = term(9 + i)
        return carry

    lax.fori_loop(0, MB, g4_body, 0)

    def slot_of(p):
        apart = (p // MB) ^ s
        level = jnp.int32(0)
        for n in range(LEVELS - 1):
            level = level + (apart == (1 << n)).astype(jnp.int32) * (n + 1)
        return level * MB + lax.rem(p, MB)

    def blocks(group):
        def body(n, carry):
            j = group * GCOLS + n
            g = pg[:, pl.ds(pl.multiple_of(j * BLOCK, BLOCK), BLOCK)]
            for k in range(NNZ):
                x = (dot(cand_t[slot_of(pat[j, k])], g) * grad_scale).astype(BF)
                row = 0
                while row < BLOCK:
                    at = k * BLOCK + row
                    piece, inner = at // 96, at % 96
                    size = min(96 - inner, BLOCK - row)
                    tb[j, piece // 2, piece % 2, inner : inner + size, :] = x[row : row + size]
                    row += size
            return carry

        lax.fori_loop(0, GCOLS, body, 0)
        view = pl.ds(group * GCOLS, GCOLS)
        return launch(tb.at[view, :, other], tb_rc.at[view], dp=d ^ 1)

    def spread(sent, received):
        return [launch(sent(chip ^ m), received(m), dp=d ^ (2 * m)) for m in CHIP_MASKS]

    def blocks_sum(group, copy):
        copy.wait_recv()

        def body(c, carry):
            for n in range(GCOLS):
                j = group * GCOLS + n
                tb_s[group, c, n] = (tb[j, c, core].astype(F32) + tb_rc[j, c].astype(F32)).astype(BF)
            return carry

        lax.fori_loop(0, CHIPS, body, 0)
        return spread(lambda c: tb_s.at[group, c], lambda m: tb_r.at[group, m])

    def flat_sum(mine, theirs, out, copy, received):
        copy.wait_recv()

        def body(c, carry):
            out[c] = (mine[c, core].astype(F32) + theirs[c].astype(F32)).astype(BF)
            return carry

        lax.fori_loop(0, CHIPS, body, 0)
        return spread(lambda c: out.at[c], lambda m: received.at[m])

    def far_relay(c):
        i, rows = part(c)
        far[c].wait_recv()
        gsend[9 + i, rows] = (g4[i, rows] + rx[12 + i, rows].astype(F32)).astype(BF)
        nears.append(launch(gsend.at[9 + i, rows], rx.at[9 + i, rows], tensor=s ^ 4))

    def flat_parts(out, t):
        for c in range(CHIPS):
            for h in range(2):
                r = (2 * c + h) * 16
                out[c, h] = t[r : r + 16]

    turned(12, 15)
    core0 = blocks(0)
    ar.step(0)
    far_relay(0)
    core1 = blocks(1)
    flat_parts(tr, (dot(codes[...].T, pg[...]) * grad_scale).astype(BF))
    core_r = launch(tr.at[:, other], tr_rc, dp=d ^ 1)
    eight0 = blocks_sum(0, core0)
    far_relay(1)
    ar.step(1)
    eight1 = blocks_sum(1, core1)
    far_relay(2)
    eight_r = flat_sum(tr, tr_rc, tr_s, core_r, tr_r)

    def g0_body(i, carry):
        g0[i] = term(i)
        return carry

    lax.fori_loop(0, MB, g0_body, 0)
    far_relay(3)
    ar.step(2)
    far_relay(4)
    far_relay(5)
    ar.step(3)
    flat_parts(tl, (dot(back[...].T, tokens()) * grad_scale).astype(BF))
    core_l = launch(tl.at[:, other], tl_rc, dp=d ^ 1)
    low = dot(back[...], left_t[...])
    for i in range(MB):
        g0[i] = g0[i] + low[:, i * BLOCK : (i + 1) * BLOCK]
    eight_l = flat_sum(tl, tl_rc, tl_s, core_l, tl_r)

    def sum_flat(own_view, received, copies, out):
        total = own_view[...].astype(F32)
        for m, c in zip(CHIP_MASKS, copies):
            c.wait_recv()
            total = total + received[m].astype(F32)
        out[...] = total

    for group, copies in ((0, eight0), (1, eight1)):
        for c in copies:
            c.wait_recv()

        def body(n, carry, group=group):
            total = tb_s[group, chip, n].astype(F32)
            for m in CHIP_MASKS:
                total = total + tb_r[group, m, n].astype(F32)
            gblk[group * GCOLS + n] = total
            return carry

        lax.fori_loop(0, GCOLS, body, 0)
    sum_flat(tr_s.at[chip], tr_r, eight_r, gright)
    for c in nears:
        c.wait_recv()
    for i in range(MB):
        total = g0[i]
        for level in (1, 2, 3, 5):
            total = total + rx[MB * level + i].astype(F32)
        gtok[:, i * BLOCK : (i + 1) * BLOCK] = total
    sum_flat(tl_s.at[chip], tl_r, eight_l, glt)
    for c in pending:
        c.wait_send()


def per_device(tokens, w_blocks, pattern, low_left, low_right, grad_out):
    grad_scale = 1.0 / math.sqrt(TOK * lax.axis_size("dp"))
    vmem = pl.BlockSpec(memory_space=pltpu.VMEM)
    hbm = pl.BlockSpec(memory_space=pltpu.HBM)
    V = pltpu.VMEM
    scratch = [
        V((COLS, NNZ, BLOCK, BLOCK), BF), pltpu.SMEM((COLS, NNZ), jnp.int32),
        V((FEAT, RANK), BF), V((RANK, HID), BF), V((TOK, HID), BF), pltpu.SemaphoreType.DMA((8,)),
        V((SLOTS, TOK, BLOCK), BF), V((SLOTS, BLOCK, TOK), BF),
        V((SLOTS, BLOCK, HID), BF), V((SLOTS, HID, BLOCK), BF),
        V((TOK, HID), F32), V((TOK, HID), BF), V((RANK, FEAT), BF), V((HID, RANK), BF),
        V((TOK, RANK), F32), V((TOK, RANK), F32), V((TOK, RANK), BF), V((TOK, RANK), BF),
        V((32, RANK), BF), V((32, RANK), BF), V((7, 32, RANK), BF), V((7, 32, RANK), BF),
        V((3, 16, 128), BF), V((3, 16, 128), BF),
        V((TOK, RANK), BF), V((TOK, RANK), BF),
        V((SLOTS, TOK, BLOCK), BF), V((SLOTS, TOK, BLOCK), BF),
        V((MB, TOK, BLOCK), F32), V((MB, TOK, BLOCK), F32),
        V((COLS, CHIPS, 2, 96, BLOCK), BF), V((COLS, CHIPS, 96, BLOCK), BF),
        V((GROUPS, CHIPS, GCOLS, 96, BLOCK), BF), V((GROUPS, CHIPS, GCOLS, 96, BLOCK), BF),
        V((CHIPS, 2, 16, HID), BF), V((CHIPS, 16, HID), BF), V((CHIPS, 16, HID), BF), V((CHIPS, 16, HID), BF),
        V((CHIPS, 2, 16, FEAT), BF), V((CHIPS, 16, FEAT), BF), V((CHIPS, 16, FEAT), BF), V((CHIPS, 16, FEAT), BF),
        pltpu.SemaphoreType.DMA((NUM_SEMS,)), pltpu.SemaphoreType.DMA((NUM_SEMS,)),
    ]
    out_shape = (
        V((TOK, HID), BF),
        V((TOK, FEAT), F32),
        V((COLS, 96, BLOCK), F32),
        V((16, FEAT), F32),
        V((16, HID), F32),
    )
    hidden, gtok, gblk, glt, gright = pl.pallas_call(
        functools.partial(kernel, grad_scale),
        name="pixelfly",
        out_shape=out_shape,
        in_specs=[hbm] * 6,
        out_specs=(vmem,) * 5,
        scratch_shapes=scratch,
        compiler_params=pltpu.CompilerParams(
            collective_id=0, has_side_effects=True, vmem_limit_bytes=56 << 20
        ),
        cost_estimate=pl.CostEstimate(flops=3 << 30, bytes_accessed=6 << 20, transcendentals=TOK * HID),
    )(tokens, w_blocks.reshape(COLS, NNZ, BLOCK, BLOCK), pattern, low_left, low_right, grad_out)
    return hidden, gtok, gblk, glt.T, gright


def solution(mesh):
    in_specs = (
        P("dp", "tensor"),
        P("tensor", None, None),
        P("tensor", None),
        P("tensor", None),
        P(None, "tensor"),
        P("dp", "tensor"),
    )
    out_specs = (
        P("dp", "tensor"),
        P("dp", "tensor"),
        P("tensor", "dp", None),
        P("tensor", "dp"),
        P("dp", "tensor"),
    )
    return jax.shard_map(
        per_device, mesh=mesh, in_specs=in_specs, out_specs=out_specs, check_vma=False
    )
```

```python
import functools
import math

import jax
import jax.numpy as jnp
from jax import lax
from jax.experimental import pallas as pl
from jax.experimental.pallas import tpu as pltpu
from jax.sharding import PartitionSpec as P

MESH = pl.DeviceIdType.MESH
BF, F32 = jnp.bfloat16, jnp.float32
BLOCK = 128
NNZ = 12
TOK = 256
MB = 3
COLS = 6
LEVELS = 6
SLOTS = MB * LEVELS
RANK = 256
HID = COLS * BLOCK
FEAT = MB * BLOCK
CHUNKS = 6
GROUPS = 2
GCOLS = COLS // GROUPS
CHIPS = 8
NEAR_GROUP = (19, 18, 17, 16, 3, 2, 1)
FAR_GROUP = (8, 4, 12)
TENSOR_PEERS = FAR_GROUP + NEAR_GROUP
CHIP_MASKS = tuple(range(1, CHIPS))
GELU_C = math.sqrt(2.0 / math.pi)
GELU_A = 0.044715


def dot(a, b):
    return jnp.dot(a, b, preferred_element_type=F32)


class Sems:
    def __init__(self, send, recv):
        self.send, self.recv, self.used = send, recv, 0

    def copy(self, src, dst, **device):
        i = self.used
        self.used += 1
        return pltpu.make_async_remote_copy(
            src_ref=src, dst_ref=dst, send_sem=self.send.at[i], recv_sem=self.recv.at[i],
            device_id=device, device_id_type=MESH,
        )


NUM_SEMS = 160


def kernel(
    grad_scale, tokens_hbm, w_hbm, pat_hbm, left_hbm, right_hbm, gout_hbm,
    hidden, gtok, gblk, glt, gright,
    w, pat, left, right, gout, load_sem,
    cand, cand_t, wd, wd_t, pre, pg, left_t, right_t,
    acc, acc2, sa_f, sa_b, sb_f, sb_b, ra_f, ra_b, rb_f, rb_b,
    codes, back, gsend, rx, g4, g0,
    tb, tb_rc, tb_s, tb_r, tr, tr_rc, tr_s, tr_r, tl, tl_rc, tl_s, tl_r,
    send_sem, recv_sem,
):
    s = lax.axis_index("tensor")
    d = lax.axis_index("dp")
    core = lax.rem(d, 2)
    chip = d // 2
    other = 1 - core
    sems = Sems(send_sem, recv_sem)
    pending = []

    def launch(src, dst, **device):
        c = sems.copy(src, dst, **device)
        c.start()
        pending.append(c)
        return c

    barrier = pltpu.get_barrier_semaphore()
    for m in TENSOR_PEERS:
        pl.semaphore_signal(barrier, inc=1, device_id={"tensor": s ^ m}, device_id_type=MESH)
    pl.semaphore_signal(barrier, inc=1, device_id={"dp": d ^ 1}, device_id_type=MESH)
    for m in CHIP_MASKS:
        pl.semaphore_signal(barrier, inc=1, device_id={"dp": d ^ (2 * m)}, device_id_type=MESH)

    def fetch(n, src, dst):
        c = pltpu.make_async_copy(src, dst, load_sem.at[n])
        c.start()
        return c

    loads = [fetch(i, tokens_hbm.at[:, pl.ds(i * BLOCK, BLOCK)], cand.at[i]) for i in range(MB)]
    loads.append(fetch(3, left_hbm, left))
    pat_load = fetch(4, pat_hbm, pat)
    w_load = fetch(5, w_hbm, w)
    right_load = fetch(6, right_hbm, right)
    gout_load = fetch(7, gout_hbm, gout)
    for c in loads:
        c.wait()

    def tokens():
        return jnp.concatenate([cand[i] for i in range(MB)], axis=1)

    acc[...] = dot(tokens(), left[...])
    sa_f[...] = acc[...].astype(BF)
    pl.semaphore_wait(barrier, len(TENSOR_PEERS) + 1 + len(CHIP_MASKS))

    def part(c):
        i, h = c // 2, c % 2
        return i, pl.ds(h * 128, 128)

    bit = lambda v, n: lax.rem(lax.shift_right_logical(v, n), 2)
    near_row = lambda v: pl.multiple_of(32 * (bit(v, 0) + 2 * bit(v, 1) + 4 * bit(v, 4)), 32)
    far_row = lambda v: pl.multiple_of(16 * bit(v, 2), 16)
    far_col = lambda v: pl.multiple_of(128 * bit(v, 3), 128)

    class AllReduce:
        def __init__(self, total, near_stage, far_stage, near_in, far_in, out):
            self.total, self.near_stage, self.far_stage = total, near_stage, far_stage
            self.near_in, self.far_in, self.out = near_in, far_in, out

        def start(self):
            self.flying = [
                launch(self.near_stage.at[pl.ds(near_row(s ^ m), 32)], self.near_in.at[n], tensor=s ^ m)
                for n, m in enumerate(NEAR_GROUP)
            ]

        def arrived(self):
            for c in self.flying:
                c.wait_recv()

        def step(self, n):
            self.arrived()
            rows = pl.ds(near_row(s), 32)
            piece = self.out.at[pl.ds(pl.multiple_of(near_row(s) + far_row(s), 16), 16), pl.ds(far_col(s), 128)]
            if n == 0:
                part = self.total[rows, :]
                for m in range(len(NEAR_GROUP)):
                    part = part + self.near_in[m].astype(F32)
                self.total[rows, :] = part
                self.far_stage[...] = part.astype(BF)
                self.flying = [
                    launch(
                        self.far_stage.at[pl.ds(far_row(s ^ m), 16), pl.ds(far_col(s ^ m), 128)],
                        self.far_in.at[i], tensor=s ^ m,
                    )
                    for i, m in enumerate(FAR_GROUP)
                ]
            elif n == 1:
                part = self.total[
                    pl.ds(pl.multiple_of(near_row(s) + far_row(s), 16), 16), pl.ds(far_col(s), 128)
                ]
                for m in range(len(FAR_GROUP)):
                    part = part + self.far_in[m].astype(F32)
                piece[...] = part.astype(BF)
                self.flying = [launch(piece, piece, tensor=s ^ m) for m in FAR_GROUP]
            elif n == 2:
                view = self.out.at[rows]
                self.flying = [launch(view, view, tensor=s ^ m) for m in NEAR_GROUP]

    four = []
    for c in range(2):
        i, rows = part(c)
        four.append(launch(cand.at[i, rows], cand.at[9 + i, rows], tensor=s ^ 4))
    ar = AllReduce(acc, sa_f, sb_f, ra_f, rb_f, codes)
    ar.start()
    for c in range(2, CHUNKS):
        i, rows = part(c)
        four.append(launch(cand.at[i, rows], cand.at[9 + i, rows], tensor=s ^ 4))
    own = cand.at[pl.ds(0, MB)]
    sixteen = launch(own, cand.at[pl.ds(15, MB)], tensor=s ^ 16)
    two = launch(own, cand.at[pl.ds(6, MB)], tensor=s ^ 2)
    one = launch(own, cand.at[pl.ds(3, MB)], tensor=s ^ 1)
    relayed = []

    def relay(c):
        i, rows = part(c)
        four[c].wait_recv()
        relayed.append(launch(cand.at[9 + i, rows], cand.at[12 + i, rows], tensor=s ^ 12))

    def dense(first, last):
        def body(slot, carry):
            level = slot // MB
            mask = lax.shift_right_logical(lax.shift_left(jnp.int32(1), level), 1)
            row = (s ^ mask) * MB + lax.rem(slot, MB)
            for j in range(COLS):
                k = jnp.int32(0)
                found = jnp.int32(0)
                for q in range(NNZ):
                    hit = pat[j, q] == row
                    k = jnp.where(hit, q, k)
                    found = jnp.where(hit, 1, found)
                block = jnp.where(found > 0, w[j, k], jnp.zeros((BLOCK, BLOCK), BF))
                wd[slot, :, j * BLOCK : (j + 1) * BLOCK] = block
                wd_t[slot, j * BLOCK : (j + 1) * BLOCK, :] = block.T
            return carry

        lax.fori_loop(first, last, body, 0)

    def turned(first, last):
        def body(slot, carry):
            cand_t[slot] = cand[slot].T
            return carry

        lax.fori_loop(first, last, body, 0)

    def forward(slots, start=None):
        def body(n, carry):
            columns = pl.ds(pl.multiple_of(n * 256, 256), 256)
            total = start(columns) if start is not None else pre[:, columns]
            for p in range(0, len(slots), 2):
                pair = slots[p : p + 2]
                x = jnp.concatenate([cand[q] for q in pair], axis=1)
                y = jnp.concatenate([wd[q, :, columns] for q in pair], axis=0)
                total = total + dot(x, y)
            pre[:, columns] = total
            return carry

        lax.fori_loop(0, HID // 256, body, 0)

    pat_load.wait()
    w_load.wait()
    dense(0, 4)
    relay(0)
    ar.step(0)
    dense(4, 8)
    relay(1)
    dense(8, 12)
    relay(2)
    ar.step(1)
    dense(12, 15)
    relay(3)
    dense(15, 18)
    right_load.wait()
    left_t[...] = left[...].T
    relay(4)
    right_t[...] = right[...].T
    turned(0, 3)
    sixteen.wait_recv()
    turned(15, 18)
    relay(5)
    ar.step(2)
    one.wait_recv()
    two.wait_recv()
    turned(3, 9)
    forward((0, 1, 2, 15, 16, 17, 3, 4, 5, 6, 7, 8), lambda columns: jnp.zeros((TOK, 256), F32))
    turned(9, 12)
    forward((9, 10, 11))
    ar.step(3)
    gout_load.wait()
    for c in range(CHUNKS):
        relayed[c].wait_recv()
    def activate(n, carry):
        columns = pl.ds(pl.multiple_of(n * 256, 256), 256)
        u = pre[:, columns]
        u = u + dot(jnp.concatenate([cand[12], cand[13]], axis=1),
                    jnp.concatenate([wd[12, :, columns], wd[13, :, columns]], axis=0))
        u = u + dot(cand[14], wd[14, :, columns])
        u = u + dot(codes[...], right[:, columns])
        uu = u * u
        t = jnp.tanh(GELU_C * (u + GELU_A * (uu * u)))
        hidden[:, columns] = (0.5 * u * (1.0 + t)).astype(BF)
        slope = 0.5 * (1.0 + t) + 0.5 * u * (1.0 - t * t) * (GELU_C * (1.0 + 3.0 * GELU_A * uu))
        pg[:, columns] = (gout[:, columns].astype(F32) * slope).astype(BF)
        return carry

    lax.fori_loop(0, HID // 256, activate, 0)

    acc2[...] = dot(pg[...], right_t[...])
    sa_b[...] = acc2[...].astype(BF)
    ar = AllReduce(acc2, sa_b, sb_b, ra_b, rb_b, back)
    ar.start()

    def term(slot):
        return dot(pg[...], wd_t[slot])

    far = []
    for i in range(MB):
        gsend[12 + i] = term(12 + i).astype(BF)
        for h in range(2):
            rows = pl.ds(h * 128, 128)
            far.append(launch(gsend.at[12 + i, rows], rx.at[12 + i, rows], tensor=s ^ 12))

    def near(level, mask):
        def body(i, carry):
            gsend[MB * level + i] = term(MB * level + i).astype(BF)
            return carry

        lax.fori_loop(0, MB, body, 0)
        view = pl.ds(MB * level, MB)
        return launch(gsend.at[view], rx.at[view], tensor=s ^ mask)

    nears = [near(5, 16), near(2, 2), near(1, 1)]

    def g4_body(i, carry):
        g4[i] = term(9 + i)
        return carry

    lax.fori_loop(0, MB, g4_body, 0)

    def slot_of(p):
        apart = (p // MB) ^ s
        level = jnp.int32(0)
        for n in range(LEVELS - 1):
            level = level + (apart == (1 << n)).astype(jnp.int32) * (n + 1)
        return level * MB + lax.rem(p, MB)

    def blocks(group):
        def body(n, carry):
            j = group * GCOLS + n
            g = pg[:, pl.ds(pl.multiple_of(j * BLOCK, BLOCK), BLOCK)]
            for k in range(NNZ):
                x = (dot(cand_t[slot_of(pat[j, k])], g) * grad_scale).astype(BF)
                row = 0
                while row < BLOCK:
                    at = k * BLOCK + row
                    piece, inner = at // 96, at % 96
                    size = min(96 - inner, BLOCK - row)
                    tb[j, piece // 2, piece % 2, inner : inner + size, :] = x[row : row + size]
                    row += size
            return carry

        lax.fori_loop(0, GCOLS, body, 0)
        view = pl.ds(group * GCOLS, GCOLS)
        return launch(tb.at[view, :, other], tb_rc.at[view], dp=d ^ 1)

    def spread(sent, received):
        return [launch(sent(chip ^ m), received(m), dp=d ^ (2 * m)) for m in CHIP_MASKS]

    def blocks_sum(group, copy):
        copy.wait_recv()

        def body(c, carry):
            for n in range(GCOLS):
                j = group * GCOLS + n
                tb_s[group, c, n] = (tb[j, c, core].astype(F32) + tb_rc[j, c].astype(F32)).astype(BF)
            return carry

        lax.fori_loop(0, CHIPS, body, 0)
        return spread(lambda c: tb_s.at[group, c], lambda m: tb_r.at[group, m])

    def flat_sum(mine, theirs, out, copy, received):
        copy.wait_recv()

        def body(c, carry):
            out[c] = (mine[c, core].astype(F32) + theirs[c].astype(F32)).astype(BF)
            return carry

        lax.fori_loop(0, CHIPS, body, 0)
        return spread(lambda c: out.at[c], lambda m: received.at[m])

    def far_relay(c):
        i, rows = part(c)
        far[c].wait_recv()
        gsend[9 + i, rows] = (g4[i, rows] + rx[12 + i, rows].astype(F32)).astype(BF)
        nears.append(launch(gsend.at[9 + i, rows], rx.at[9 + i, rows], tensor=s ^ 4))

    def flat_parts(out, t):
        for c in range(CHIPS):
            for h in range(2):
                r = (2 * c + h) * 16
                out[c, h] = t[r : r + 16]

    turned(12, 15)
    core0 = blocks(0)
    ar.step(0)
    far_relay(0)
    core1 = blocks(1)
    flat_parts(tr, (dot(codes[...].T, pg[...]) * grad_scale).astype(BF))
    core_r = launch(tr.at[:, other], tr_rc, dp=d ^ 1)
    eight0 = blocks_sum(0, core0)
    far_relay(1)
    ar.step(1)
    eight1 = blocks_sum(1, core1)
    far_relay(2)
    eight_r = flat_sum(tr, tr_rc, tr_s, core_r, tr_r)

    def g0_body(i, carry):
        g0[i] = term(i)
        return carry

    lax.fori_loop(0, MB, g0_body, 0)
    far_relay(3)
    ar.step(2)
    far_relay(4)
    far_relay(5)
    ar.step(3)
    early = list(pending)
    flat_parts(tl, (dot(back[...].T, tokens()) * grad_scale).astype(BF))
    core_l = launch(tl.at[:, other], tl_rc, dp=d ^ 1)
    low = dot(back[...], left_t[...])
    for i in range(MB):
        g0[i] = g0[i] + low[:, i * BLOCK : (i + 1) * BLOCK]
    eight_l = flat_sum(tl, tl_rc, tl_s, core_l, tl_r)

    def sum_flat(own_view, received, copies, out):
        total = own_view[...].astype(F32)
        for m, c in zip(CHIP_MASKS, copies):
            c.wait_recv()
            total = total + received[m].astype(F32)
        out[...] = total

    for group, copies in ((0, eight0), (1, eight1)):
        for c in copies:
            c.wait_recv()

        def body(n, carry, group=group):
            total = tb_s[group, chip, n].astype(F32)
            for m in CHIP_MASKS:
                total = total + tb_r[group, m, n].astype(F32)
            gblk[group * GCOLS + n] = total
            return carry

        lax.fori_loop(0, GCOLS, body, 0)
    sum_flat(tr_s.at[chip], tr_r, eight_r, gright)
    for c in nears:
        c.wait_recv()
    for i in range(MB):
        total = g0[i]
        for level in (1, 2, 3, 5):
            total = total + rx[MB * level + i].astype(F32)
        gtok[:, i * BLOCK : (i + 1) * BLOCK] = total
    for c in early:
        c.wait_send()
    sum_flat(tl_s.at[chip], tl_r, eight_l, glt)
    for c in pending[len(early):]:
        c.wait_send()


def per_device(tokens, w_blocks, pattern, low_left, low_right, grad_out):
    grad_scale = 1.0 / math.sqrt(TOK * lax.axis_size("dp"))
    vmem = pl.BlockSpec(memory_space=pltpu.VMEM)
    hbm = pl.BlockSpec(memory_space=pltpu.HBM)
    V = pltpu.VMEM
    scratch = [
        V((COLS, NNZ, BLOCK, BLOCK), BF), pltpu.SMEM((COLS, NNZ), jnp.int32),
        V((FEAT, RANK), BF), V((RANK, HID), BF), V((TOK, HID), BF), pltpu.SemaphoreType.DMA((8,)),
        V((SLOTS, TOK, BLOCK), BF), V((SLOTS, BLOCK, TOK), BF),
        V((SLOTS, BLOCK, HID), BF), V((SLOTS, HID, BLOCK), BF),
        V((TOK, HID), F32), V((TOK, HID), BF), V((RANK, FEAT), BF), V((HID, RANK), BF),
        V((TOK, RANK), F32), V((TOK, RANK), F32), V((TOK, RANK), BF), V((TOK, RANK), BF),
        V((32, RANK), BF), V((32, RANK), BF), V((7, 32, RANK), BF), V((7, 32, RANK), BF),
        V((3, 16, 128), BF), V((3, 16, 128), BF),
        V((TOK, RANK), BF), V((TOK, RANK), BF),
        V((SLOTS, TOK, BLOCK), BF), V((SLOTS, TOK, BLOCK), BF),
        V((MB, TOK, BLOCK), F32), V((MB, TOK, BLOCK), F32),
        V((COLS, CHIPS, 2, 96, BLOCK), BF), V((COLS, CHIPS, 96, BLOCK), BF),
        V((GROUPS, CHIPS, GCOLS, 96, BLOCK), BF), V((GROUPS, CHIPS, GCOLS, 96, BLOCK), BF),
        V((CHIPS, 2, 16, HID), BF), V((CHIPS, 16, HID), BF), V((CHIPS, 16, HID), BF), V((CHIPS, 16, HID), BF),
        V((CHIPS, 2, 16, FEAT), BF), V((CHIPS, 16, FEAT), BF), V((CHIPS, 16, FEAT), BF), V((CHIPS, 16, FEAT), BF),
        pltpu.SemaphoreType.DMA((NUM_SEMS,)), pltpu.SemaphoreType.DMA((NUM_SEMS,)),
    ]
    out_shape = (
        V((TOK, HID), BF),
        V((TOK, FEAT), F32),
        V((COLS, 96, BLOCK), F32),
        V((16, FEAT), F32),
        V((16, HID), F32),
    )
    hidden, gtok, gblk, glt, gright = pl.pallas_call(
        functools.partial(kernel, grad_scale),
        name="pixelfly",
        out_shape=out_shape,
        in_specs=[hbm] * 6,
        out_specs=(vmem,) * 5,
        scratch_shapes=scratch,
        compiler_params=pltpu.CompilerParams(
            collective_id=0, has_side_effects=True, vmem_limit_bytes=56 << 20
        ),
        cost_estimate=pl.CostEstimate(flops=3 << 30, bytes_accessed=6 << 20, transcendentals=TOK * HID),
    )(tokens, w_blocks.reshape(COLS, NNZ, BLOCK, BLOCK), pattern, low_left, low_right, grad_out)
    return hidden, gtok, gblk, glt.T, gright


def solution(mesh):
    in_specs = (
        P("dp", "tensor"),
        P("tensor", None, None),
        P("tensor", None),
        P("tensor", None),
        P(None, "tensor"),
        P("dp", "tensor"),
    )
    out_specs = (
        P("dp", "tensor"),
        P("dp", "tensor"),
        P("tensor", "dp", None),
        P("tensor", "dp"),
        P("dp", "tensor"),
    )
    return jax.shard_map(
        per_device, mesh=mesh, in_specs=in_specs, out_specs=out_specs, check_vma=False
    )
```

```python
import functools
import math

import jax
import jax.numpy as jnp
from jax import lax
from jax.experimental import pallas as pl
from jax.experimental.pallas import tpu as pltpu
from jax.sharding import PartitionSpec as P

MESH = pl.DeviceIdType.MESH
BF, F32 = jnp.bfloat16, jnp.float32
BLOCK = 128
NNZ = 12
TOK = 256
MB = 3
COLS = 6
LEVELS = 6
SLOTS = MB * LEVELS
RANK = 256
HID = COLS * BLOCK
FEAT = MB * BLOCK
CHUNKS = 6
GROUPS = 2
GCOLS = COLS // GROUPS
CHIPS = 8
NEAR_GROUP = (19, 18, 17, 16, 3, 2, 1)
FAR_GROUP = (8, 4, 12)
TENSOR_PEERS = FAR_GROUP + NEAR_GROUP
CHIP_MASKS = tuple(range(1, CHIPS))
GELU_C = math.sqrt(2.0 / math.pi)
GELU_A = 0.044715


def dot(a, b):
    return jnp.dot(a, b, preferred_element_type=F32)


class Sems:
    def __init__(self, send, recv):
        self.send, self.recv, self.used = send, recv, 0

    def copy(self, src, dst, **device):
        i = self.used
        self.used += 1
        return pltpu.make_async_remote_copy(
            src_ref=src, dst_ref=dst, send_sem=self.send.at[i], recv_sem=self.recv.at[i],
            device_id=device, device_id_type=MESH,
        )


NUM_SEMS = 160


def kernel(
    grad_scale, tokens_hbm, w_hbm, pat_hbm, left_hbm, right_hbm, gout_hbm,
    hidden, gtok, gblk, glt, gright,
    w, pat, left, right, gout, load_sem,
    cand, cand_t, wd, wd_t, pre, pg, left_t, right_t,
    acc, acc2, sa_f, sa_b, sb_f, sb_b, ra_f, ra_b, rb_f, rb_b,
    codes, back, gsend, rx, g4, g0,
    tb, tb_rc, tb_s, tb_r, tr, tr_rc, tr_s, tr_r, tl, tl_rc, tl_s, tl_r,
    send_sem, recv_sem,
):
    s = lax.axis_index("tensor")
    d = lax.axis_index("dp")
    core = lax.rem(d, 2)
    chip = d // 2
    other = 1 - core
    sems = Sems(send_sem, recv_sem)
    pending = []

    def launch(src, dst, **device):
        c = sems.copy(src, dst, **device)
        c.start()
        pending.append(c)
        return c

    barrier = pltpu.get_barrier_semaphore()
    for m in TENSOR_PEERS:
        pl.semaphore_signal(barrier, inc=1, device_id={"tensor": s ^ m}, device_id_type=MESH)
    pl.semaphore_signal(barrier, inc=1, device_id={"dp": d ^ 1}, device_id_type=MESH)
    for m in CHIP_MASKS:
        pl.semaphore_signal(barrier, inc=1, device_id={"dp": d ^ (2 * m)}, device_id_type=MESH)

    def fetch(n, src, dst):
        c = pltpu.make_async_copy(src, dst, load_sem.at[n])
        c.start()
        return c

    loads = [fetch(i, tokens_hbm.at[:, pl.ds(i * BLOCK, BLOCK)], cand.at[i]) for i in range(MB)]
    loads.append(fetch(3, left_hbm, left))
    pat_load = fetch(4, pat_hbm, pat)
    w_load = fetch(5, w_hbm, w)
    right_load = fetch(6, right_hbm, right)
    gout_load = fetch(7, gout_hbm, gout)
    for c in loads:
        c.wait()

    def tokens():
        return jnp.concatenate([cand[i] for i in range(MB)], axis=1)

    acc[...] = dot(tokens(), left[...])
    sa_f[...] = acc[...].astype(BF)
    pl.semaphore_wait(barrier, len(TENSOR_PEERS) + 1 + len(CHIP_MASKS))

    def part(c):
        i, h = c // 2, c % 2
        return i, pl.ds(h * 128, 128)

    bit = lambda v, n: lax.rem(lax.shift_right_logical(v, n), 2)
    near_row = lambda v: pl.multiple_of(32 * (bit(v, 0) + 2 * bit(v, 1) + 4 * bit(v, 4)), 32)
    far_row = lambda v: pl.multiple_of(16 * bit(v, 2), 16)
    far_col = lambda v: pl.multiple_of(128 * bit(v, 3), 128)

    class AllReduce:
        def __init__(self, total, near_stage, far_stage, near_in, far_in, out):
            self.total, self.near_stage, self.far_stage = total, near_stage, far_stage
            self.near_in, self.far_in, self.out = near_in, far_in, out

        def start(self):
            self.flying = [
                launch(self.near_stage.at[pl.ds(near_row(s ^ m), 32)], self.near_in.at[n], tensor=s ^ m)
                for n, m in enumerate(NEAR_GROUP)
            ]

        def arrived(self):
            for c in self.flying:
                c.wait_recv()

        def step(self, n):
            self.arrived()
            rows = pl.ds(near_row(s), 32)
            piece = self.out.at[pl.ds(pl.multiple_of(near_row(s) + far_row(s), 16), 16), pl.ds(far_col(s), 128)]
            if n == 0:
                part = self.total[rows, :]
                for m in range(len(NEAR_GROUP)):
                    part = part + self.near_in[m].astype(F32)
                self.total[rows, :] = part
                self.far_stage[...] = part.astype(BF)
                self.flying = [
                    launch(
                        self.far_stage.at[pl.ds(far_row(s ^ m), 16), pl.ds(far_col(s ^ m), 128)],
                        self.far_in.at[i], tensor=s ^ m,
                    )
                    for i, m in enumerate(FAR_GROUP)
                ]
            elif n == 1:
                part = self.total[
                    pl.ds(pl.multiple_of(near_row(s) + far_row(s), 16), 16), pl.ds(far_col(s), 128)
                ]
                for m in range(len(FAR_GROUP)):
                    part = part + self.far_in[m].astype(F32)
                piece[...] = part.astype(BF)
                self.flying = [launch(piece, piece, tensor=s ^ m) for m in FAR_GROUP]
            elif n == 2:
                view = self.out.at[rows]
                self.flying = [launch(view, view, tensor=s ^ m) for m in NEAR_GROUP]

    ar = AllReduce(acc, sa_f, sb_f, ra_f, rb_f, codes)
    ar.start()
    four = []
    for c in range(CHUNKS):
        i, rows = part(c)
        four.append(launch(cand.at[i, rows], cand.at[9 + i, rows], tensor=s ^ 4))
    own = cand.at[pl.ds(0, MB)]
    sixteen = launch(own, cand.at[pl.ds(15, MB)], tensor=s ^ 16)
    two = launch(own, cand.at[pl.ds(6, MB)], tensor=s ^ 2)
    one = launch(own, cand.at[pl.ds(3, MB)], tensor=s ^ 1)
    relayed = []

    def relay(c):
        i, rows = part(c)
        four[c].wait_recv()
        relayed.append(launch(cand.at[9 + i, rows], cand.at[12 + i, rows], tensor=s ^ 12))

    def dense(first, last):
        def body(slot, carry):
            level = slot // MB
            mask = lax.shift_right_logical(lax.shift_left(jnp.int32(1), level), 1)
            row = (s ^ mask) * MB + lax.rem(slot, MB)
            for j in range(COLS):
                k = jnp.int32(0)
                found = jnp.int32(0)
                for q in range(NNZ):
                    hit = pat[j, q] == row
                    k = jnp.where(hit, q, k)
                    found = jnp.where(hit, 1, found)
                block = jnp.where(found > 0, w[j, k], jnp.zeros((BLOCK, BLOCK), BF))
                wd[slot, :, j * BLOCK : (j + 1) * BLOCK] = block
                wd_t[slot, j * BLOCK : (j + 1) * BLOCK, :] = block.T
            return carry

        lax.fori_loop(first, last, body, 0)

    def turned(first, last):
        def body(slot, carry):
            cand_t[slot] = cand[slot].T
            return carry

        lax.fori_loop(first, last, body, 0)

    def forward(slots, start=None):
        def body(n, carry):
            columns = pl.ds(pl.multiple_of(n * 256, 256), 256)
            total = start(columns) if start is not None else pre[:, columns]
            for p in range(0, len(slots), 2):
                pair = slots[p : p + 2]
                x = jnp.concatenate([cand[q] for q in pair], axis=1)
                y = jnp.concatenate([wd[q, :, columns] for q in pair], axis=0)
                total = total + dot(x, y)
            pre[:, columns] = total
            return carry

        lax.fori_loop(0, HID // 256, body, 0)

    pat_load.wait()
    w_load.wait()
    dense(0, 4)
    relay(0)
    ar.step(0)
    dense(4, 8)
    relay(1)
    dense(8, 12)
    relay(2)
    ar.step(1)
    dense(12, 15)
    relay(3)
    dense(15, 18)
    right_load.wait()
    left_t[...] = left[...].T
    relay(4)
    right_t[...] = right[...].T
    turned(0, 3)
    sixteen.wait_recv()
    turned(15, 18)
    relay(5)
    ar.step(2)
    one.wait_recv()
    two.wait_recv()
    turned(3, 9)
    forward((0, 1, 2, 15, 16, 17, 3, 4, 5, 6, 7, 8), lambda columns: jnp.zeros((TOK, 256), F32))
    turned(9, 12)
    forward((9, 10, 11))
    ar.step(3)
    gout_load.wait()
    for c in range(CHUNKS):
        relayed[c].wait_recv()
    def activate(n, carry):
        columns = pl.ds(pl.multiple_of(n * 256, 256), 256)
        u = pre[:, columns]
        u = u + dot(jnp.concatenate([cand[12], cand[13]], axis=1),
                    jnp.concatenate([wd[12, :, columns], wd[13, :, columns]], axis=0))
        u = u + dot(cand[14], wd[14, :, columns])
        u = u + dot(codes[...], right[:, columns])
        uu = u * u
        t = jnp.tanh(GELU_C * (u + GELU_A * (uu * u)))
        hidden[:, columns] = (0.5 * u * (1.0 + t)).astype(BF)
        slope = 0.5 * (1.0 + t) + 0.5 * u * (1.0 - t * t) * (GELU_C * (1.0 + 3.0 * GELU_A * uu))
        pg[:, columns] = (gout[:, columns].astype(F32) * slope).astype(BF)
        return carry

    lax.fori_loop(0, HID // 256, activate, 0)

    acc2[...] = dot(pg[...], right_t[...])
    sa_b[...] = acc2[...].astype(BF)
    ar = AllReduce(acc2, sa_b, sb_b, ra_b, rb_b, back)
    ar.start()

    def term(slot):
        return dot(pg[...], wd_t[slot])

    far = []
    for i in range(MB):
        gsend[12 + i] = term(12 + i).astype(BF)
        for h in range(2):
            rows = pl.ds(h * 128, 128)
            far.append(launch(gsend.at[12 + i, rows], rx.at[12 + i, rows], tensor=s ^ 12))

    def near(level, mask):
        def body(i, carry):
            gsend[MB * level + i] = term(MB * level + i).astype(BF)
            return carry

        lax.fori_loop(0, MB, body, 0)
        view = pl.ds(MB * level, MB)
        return launch(gsend.at[view], rx.at[view], tensor=s ^ mask)

    nears = [near(5, 16), near(2, 2), near(1, 1)]

    def g4_body(i, carry):
        g4[i] = term(9 + i)
        return carry

    lax.fori_loop(0, MB, g4_body, 0)

    def slot_of(p):
        apart = (p // MB) ^ s
        level = jnp.int32(0)
        for n in range(LEVELS - 1):
            level = level + (apart == (1 << n)).astype(jnp.int32) * (n + 1)
        return level * MB + lax.rem(p, MB)

    def blocks(group):
        def body(n, carry):
            j = group * GCOLS + n
            g = pg[:, pl.ds(pl.multiple_of(j * BLOCK, BLOCK), BLOCK)]
            for k in range(NNZ):
                x = (dot(cand_t[slot_of(pat[j, k])], g) * grad_scale).astype(BF)
                row = 0
                while row < BLOCK:
                    at = k * BLOCK + row
                    piece, inner = at // 96, at % 96
                    size = min(96 - inner, BLOCK - row)
                    tb[j, piece // 2, piece % 2, inner : inner + size, :] = x[row : row + size]
                    row += size
            return carry

        lax.fori_loop(0, GCOLS, body, 0)
        view = pl.ds(group * GCOLS, GCOLS)
        return launch(tb.at[view, :, other], tb_rc.at[view], dp=d ^ 1)

    def spread(sent, received):
        return [launch(sent(chip ^ m), received(m), dp=d ^ (2 * m)) for m in CHIP_MASKS]

    def blocks_sum(group, copy):
        copy.wait_recv()

        def body(c, carry):
            for n in range(GCOLS):
                j = group * GCOLS + n
                tb_s[group, c, n] = (tb[j, c, core].astype(F32) + tb_rc[j, c].astype(F32)).astype(BF)
            return carry

        lax.fori_loop(0, CHIPS, body, 0)
        return spread(lambda c: tb_s.at[group, c], lambda m: tb_r.at[group, m])

    def flat_sum(mine, theirs, out, copy, received):
        copy.wait_recv()

        def body(c, carry):
            out[c] = (mine[c, core].astype(F32) + theirs[c].astype(F32)).astype(BF)
            return carry

        lax.fori_loop(0, CHIPS, body, 0)
        return spread(lambda c: out.at[c], lambda m: received.at[m])

    def far_relay(c):
        i, rows = part(c)
        far[c].wait_recv()
        gsend[9 + i, rows] = (g4[i, rows] + rx[12 + i, rows].astype(F32)).astype(BF)
        nears.append(launch(gsend.at[9 + i, rows], rx.at[9 + i, rows], tensor=s ^ 4))

    def flat_parts(out, t):
        for c in range(CHIPS):
            for h in range(2):
                r = (2 * c + h) * 16
                out[c, h] = t[r : r + 16]

    turned(12, 15)
    core0 = blocks(0)
    ar.step(0)
    far_relay(0)
    core1 = blocks(1)
    flat_parts(tr, (dot(codes[...].T, pg[...]) * grad_scale).astype(BF))
    core_r = launch(tr.at[:, other], tr_rc, dp=d ^ 1)
    eight0 = blocks_sum(0, core0)
    far_relay(1)
    ar.step(1)
    eight1 = blocks_sum(1, core1)
    far_relay(2)
    eight_r = flat_sum(tr, tr_rc, tr_s, core_r, tr_r)

    def g0_body(i, carry):
        g0[i] = term(i)
        return carry

    lax.fori_loop(0, MB, g0_body, 0)
    far_relay(3)
    ar.step(2)
    far_relay(4)
    far_relay(5)
    ar.step(3)
    early = list(pending)
    flat_parts(tl, (dot(back[...].T, tokens()) * grad_scale).astype(BF))
    core_l = launch(tl.at[:, other], tl_rc, dp=d ^ 1)
    low = dot(back[...], left_t[...])
    for i in range(MB):
        g0[i] = g0[i] + low[:, i * BLOCK : (i + 1) * BLOCK]
    eight_l = flat_sum(tl, tl_rc, tl_s, core_l, tl_r)

    def sum_flat(own_view, received, copies, out):
        total = own_view[...].astype(F32)
        for m, c in zip(CHIP_MASKS, copies):
            c.wait_recv()
            total = total + received[m].astype(F32)
        out[...] = total

    for group, copies in ((0, eight0), (1, eight1)):
        for c in copies:
            c.wait_recv()

        def body(n, carry, group=group):
            total = tb_s[group, chip, n].astype(F32)
            for m in CHIP_MASKS:
                total = total + tb_r[group, m, n].astype(F32)
            gblk[group * GCOLS + n] = total
            return carry

        lax.fori_loop(0, GCOLS, body, 0)
    sum_flat(tr_s.at[chip], tr_r, eight_r, gright)
    for c in nears:
        c.wait_recv()
    for i in range(MB):
        total = g0[i]
        for level in (1, 2, 3, 5):
            total = total + rx[MB * level + i].astype(F32)
        gtok[:, i * BLOCK : (i + 1) * BLOCK] = total
    for c in early:
        c.wait_send()
    sum_flat(tl_s.at[chip], tl_r, eight_l, glt)
    for c in pending[len(early):]:
        c.wait_send()


def per_device(tokens, w_blocks, pattern, low_left, low_right, grad_out):
    grad_scale = 1.0 / math.sqrt(TOK * lax.axis_size("dp"))
    vmem = pl.BlockSpec(memory_space=pltpu.VMEM)
    hbm = pl.BlockSpec(memory_space=pltpu.HBM)
    V = pltpu.VMEM
    scratch = [
        V((COLS, NNZ, BLOCK, BLOCK), BF), pltpu.SMEM((COLS, NNZ), jnp.int32),
        V((FEAT, RANK), BF), V((RANK, HID), BF), V((TOK, HID), BF), pltpu.SemaphoreType.DMA((8,)),
        V((SLOTS, TOK, BLOCK), BF), V((SLOTS, BLOCK, TOK), BF),
        V((SLOTS, BLOCK, HID), BF), V((SLOTS, HID, BLOCK), BF),
        V((TOK, HID), F32), V((TOK, HID), BF), V((RANK, FEAT), BF), V((HID, RANK), BF),
        V((TOK, RANK), F32), V((TOK, RANK), F32), V((TOK, RANK), BF), V((TOK, RANK), BF),
        V((32, RANK), BF), V((32, RANK), BF), V((7, 32, RANK), BF), V((7, 32, RANK), BF),
        V((3, 16, 128), BF), V((3, 16, 128), BF),
        V((TOK, RANK), BF), V((TOK, RANK), BF),
        V((SLOTS, TOK, BLOCK), BF), V((SLOTS, TOK, BLOCK), BF),
        V((MB, TOK, BLOCK), F32), V((MB, TOK, BLOCK), F32),
        V((COLS, CHIPS, 2, 96, BLOCK), BF), V((COLS, CHIPS, 96, BLOCK), BF),
        V((GROUPS, CHIPS, GCOLS, 96, BLOCK), BF), V((GROUPS, CHIPS, GCOLS, 96, BLOCK), BF),
        V((CHIPS, 2, 16, HID), BF), V((CHIPS, 16, HID), BF), V((CHIPS, 16, HID), BF), V((CHIPS, 16, HID), BF),
        V((CHIPS, 2, 16, FEAT), BF), V((CHIPS, 16, FEAT), BF), V((CHIPS, 16, FEAT), BF), V((CHIPS, 16, FEAT), BF),
        pltpu.SemaphoreType.DMA((NUM_SEMS,)), pltpu.SemaphoreType.DMA((NUM_SEMS,)),
    ]
    out_shape = (
        V((TOK, HID), BF),
        V((TOK, FEAT), F32),
        V((COLS, 96, BLOCK), F32),
        V((16, FEAT), F32),
        V((16, HID), F32),
    )
    hidden, gtok, gblk, glt, gright = pl.pallas_call(
        functools.partial(kernel, grad_scale),
        name="pixelfly",
        out_shape=out_shape,
        in_specs=[hbm] * 6,
        out_specs=(vmem,) * 5,
        scratch_shapes=scratch,
        compiler_params=pltpu.CompilerParams(
            collective_id=0, has_side_effects=True, vmem_limit_bytes=56 << 20
        ),
        cost_estimate=pl.CostEstimate(flops=3 << 30, bytes_accessed=6 << 20, transcendentals=TOK * HID),
    )(tokens, w_blocks.reshape(COLS, NNZ, BLOCK, BLOCK), pattern, low_left, low_right, grad_out)
    return hidden, gtok, gblk, glt.T, gright


def solution(mesh):
    in_specs = (
        P("dp", "tensor"),
        P("tensor", None, None),
        P("tensor", None),
        P("tensor", None),
        P(None, "tensor"),
        P("dp", "tensor"),
    )
    out_specs = (
        P("dp", "tensor"),
        P("dp", "tensor"),
        P("tensor", "dp", None),
        P("tensor", "dp"),
        P("dp", "tensor"),
    )
    return jax.shard_map(
        per_device, mesh=mesh, in_specs=in_specs, out_specs=out_specs, check_vma=False
    )
```
